32 devices in a mesh: section: 2 (over x), seq: 8 (over z, y), head: 2 (over core).
Axes of the slice: x: 2, y: 2, z: 4, core: 2. Of those that a mesh axis runs over, the one named last changes fastest.
Arguments:
- query_nope: bfloat16 [2, 1024, 64, 128], P('section', 'seq', 'head'), may hold values from -6 to 6
- query_rope: bfloat16 [2, 1024, 4096], P('section', 'seq', 'head'), may hold values from -8 to 8
- latent: bfloat16 [2, 1024, 576], P('section', ('seq', 'head')), may hold values from -8 to 8
- up_key: bfloat16 [64, 512, 128], P('head'), may hold values from -0.25 to 0.25
- value_up_weight: bfloat16 [64, 512, 128], P('head'), may hold values from -1.5 to 1.5
- lengths: int32 [4], replicated, may hold values from 1 to 640, 1024 in all
- owner_request_table: int32 [32], replicated, may hold values from 0 to 31, each once
Outputs:
- attended: bfloat16 [2, 1024, 64, 128], P('section', 'seq', 'head')
The draws below stay inside these ranges and needn't reach their ends.
Inputs may be any that keep to these rules, and one draw needn't show every extreme that they name: The 4 lengths sum to 1024; one is exactly 640. `owner_request_table`: every request 0 to 31 appears once.
All inputs are finite; a program needn't handle non-finite values.
Results may differ from the reference program's by a relative error of at most 0.0075.
Values may be sent and summed in bfloat16 or wider, within the bound.
No kernel may reach another device: no remote copies, remote signals or barrier semaphores. Data moves between devices by JAX's collectives and lax.ppermute only.
A program may use at most 128 MiB of HBM per device.

```python
import math
import jax
import jax.numpy as jnp
import numpy as np
from jax import lax

HEADS = 64
KV_RANK = 512
ROPE_DIM = 64
NOPE_DIM = 128
V_DIM = 128
SAMPLES = 8
STEPS = 4
BLOCK = 64
TOK_DEV = 128
TOKENS = 1024
PROMPTS = 4
REQUESTS = 32
GROUPS = 8
LEN_MOST = 640
N_SEQ = 8


def draw_latent(key, part):
    key = jax.random.fold_in(key, 3)
    starting_sample = jnp.clip(jax.random.normal(key, (2, TOKENS, KV_RANK + ROPE_DIM), jnp.float32), -6.0, 6.0)
    return starting_sample.astype(jnp.bfloat16)


def draw_query_rope(key, part):
    key = jax.random.fold_in(key, 5)
    starting_sample = jnp.clip(jax.random.normal(key, (2, TOKENS, HEADS, ROPE_DIM), jnp.float32), -6.0, 6.0)
    return starting_sample.reshape(2, TOKENS, HEADS * ROPE_DIM).astype(jnp.bfloat16)


def block_levels(stream_key, extent, pieces, smallest, top_value):
    def one(axis_at, shards_of):
        heights = jax.random.uniform(jax.random.fold_in(jax.random.fold_in(stream_key, 6), axis_at), (shards_of,), jnp.float32, smallest / len(pieces), top_value / len(pieces))
        return jnp.repeat(jnp.exp(heights), extent[axis_at] // shards_of).reshape((-1,) + (1,) * (len(extent) - axis_at - 1))

    level = one(*pieces[0])
    for cut in pieces[1:]:
        level = level * one(*cut)
    return level


def length_profile(number_of, total, most, slope):
    portions = [(1 << 20) // math.isqrt(rank ** slope) + 1 for rank in range(2, number_of + 1)]
    spare, holding = total - most - (number_of - 1), [1] * (number_of - 1)
    while spare > 0:
        free = [i for i in range(number_of - 1) if holding[i] < most]
        mass, left = sum([portions[i] for i in free]), spare
        for i in free:
            extra = min(most - holding[i], max(1, left * portions[i] // mass), spare)
            holding[i] = holding[i] + extra
            spare = spare - extra
    return np.array([most] + holding)


def ragged(stream_key, amount, total, most, slope):
    if amount == 2:
        one = jax.random.randint(stream_key, (), max(1, total - most), min(most, total - 1) + 1)
        return jnp.stack([one, total - one])
    sizes = jnp.asarray(length_profile(amount, total, most, slope), jnp.int32)
    pairs = (amount - 1) // 2
    giver, sink = sizes[1:1 + 2 * pairs:2], sizes[2:2 + 2 * pairs:2]
    room = jnp.minimum(giver - 1, most - sink)
    shifted = jax.random.randint(jax.random.fold_in(stream_key, 1), (pairs,), 0, 1 << 20) % (room + 1)
    sizes = sizes.at[1:1 + 2 * pairs:2].set(giver - shifted).at[2:2 + 2 * pairs:2].set(sink + shifted)
    return sizes[jax.random.permutation(jax.random.fold_in(stream_key, 2), amount)]


def centred(own_key, extent, width, bound, split=(), kind=jnp.bfloat16):
    result = jax.random.normal(own_key, extent, jnp.float32) * width
    if len(split) > 0:
        result = block_levels(own_key, extent, split, -0.22, 0.18) * result
    return jnp.clip(result, min=-bound, max=bound).astype(kind)


def setup_inputs(seed: int = 0) -> dict:
    seeds = jax.random.split(jax.random.key(seed), 8)
    return {
        "query_nope": centred(seeds[0], (2, TOKENS, HEADS, NOPE_DIM), 1.0, 6.0, ((0, 2), (1, 8), (2, 2))),
        "query_rope": draw_query_rope(jax.random.fold_in(seeds[7], 71), 0),
        "latent": draw_latent(jax.random.fold_in(seeds[7], 71), 0),
        "up_key": centred(seeds[3], (HEADS, KV_RANK, NOPE_DIM), KV_RANK ** -0.5, 0.25, ((0, 2),)),
        "value_up_weight": centred(seeds[4], (HEADS, KV_RANK, V_DIM), 0.25, 1.5, ((0, 2),)),
        "lengths": ragged(seeds[5], PROMPTS, TOKENS, LEN_MOST, 2).astype(jnp.int32),
        "owner_request_table": jax.random.permutation(seeds[6], REQUESTS).astype(jnp.int32),
    }


scale_top = 448.0
tiny_eps = 1e-06
masked_low = -1e+30

def absorb(part_nope, part_rope, up_key):
    row_count = part_rope.shape[0]
    lifted = jnp.einsum('thn,hkn->thk', part_nope.astype(jnp.float32), up_key.astype(jnp.float32))
    rope_part = part_rope.reshape(row_count, HEADS, ROPE_DIM).astype(jnp.float32)
    joined = jnp.concatenate([lifted, rope_part], axis=2).astype(jnp.bfloat16)
    return joined.reshape(row_count * HEADS, KV_RANK + ROPE_DIM)

def quantize(row_data):
    blocks = row_data.astype(jnp.float32).reshape(-1, BLOCK, row_data.shape[1])
    largest = lax.optimization_barrier(jnp.max(jnp.abs(blocks), axis=(1, 2)))
    block_scale = ((largest + tiny_eps) / scale_top).astype(jnp.bfloat16)
    stored = (blocks / block_scale.astype(jnp.float32)[:, None, None]).astype(jnp.bfloat16)
    return (stored.reshape(row_data.shape), jnp.repeat(block_scale, BLOCK))

def token_start(positions, starts):
    return lax.optimization_barrier(jnp.max(jnp.where(starts[None, :] <= positions[:, None], starts[None, :], 0), axis=1)).astype(jnp.int32)

def attend(queries, key_rows, scales, visible):
    soft_scale = 1.0 / math.sqrt(NOPE_DIM + ROPE_DIM)
    factor = scales.astype(jnp.float32)
    scores = jnp.dot(queries, key_rows.T, preferred_element_type=jnp.float32)
    scores = scores * (factor * soft_scale)[None, :]
    masked = jnp.where(visible, scores, masked_low)
    row_top = lax.optimization_barrier(jnp.max(masked, axis=1))
    expo_terms = jnp.where(visible, jnp.exp(masked - row_top[:, None]), 0.0)
    weights = (expo_terms * factor[None, :]).astype(jnp.bfloat16)
    summed = jnp.dot(weights, key_rows[:, :KV_RANK], preferred_element_type=jnp.float32)
    return (summed / lax.optimization_barrier(jnp.sum(expo_terms, axis=1))[:, None]).astype(jnp.bfloat16)

def project(latent_result, value_up_weight, row_count):
    reshaped_rows = latent_result.reshape(row_count, HEADS, KV_RANK).astype(jnp.float32)
    return jnp.einsum('ryb,ybw->ryw', reshaped_rows, value_up_weight.astype(jnp.float32)).astype(jnp.bfloat16)

def reference(query_nope, query_rope, latent, up_key, value_up_weight, lengths, owner_request_table):
    prompt_ends = jnp.cumsum(lengths).astype(jnp.int32)
    starts = (prompt_ends - lengths).astype(jnp.int32)
    stored, key_scale = quantize(latent[0])
    band_rows = STEPS * SAMPLES
    short_window = 4 * TOK_DEV

    def prefill_block(block_index):
        first_row = block_index * TOK_DEV
        positions = first_row + jnp.arange(TOK_DEV, dtype=jnp.int32)
        queries = absorb(lax.dynamic_slice_in_dim(query_nope[0], first_row, TOK_DEV, 0), lax.dynamic_slice_in_dim(query_rope[0], first_row, TOK_DEV, 0), up_key)
        prompt_low = token_start(positions, starts)
        reach = first_row + TOK_DEV - prompt_low[0]

        def windowed(window):

            def run_window(unused):
                window_start = jnp.clip(prompt_low[0], 0, TOKENS - window).astype(jnp.int32)
                key_rows = lax.dynamic_slice_in_dim(stored, window_start, window, 0)
                scales = lax.dynamic_slice_in_dim(key_scale, window_start, window, 0)
                key_spots = window_start + jnp.arange(window, dtype=jnp.int32)
                visible = (key_spots[None, :] >= prompt_low[:, None]) & (key_spots[None, :] <= positions[:, None])
                return attend(queries, key_rows, scales, jnp.repeat(visible, HEADS, axis=0))
            return run_window
        latent_result = lax.cond(reach <= short_window, windowed(short_window), windowed(LEN_MOST + TOK_DEV), 0)
        return project(latent_result, value_up_weight, TOK_DEV)

    def decode_request(request_index):
        first_row = request_index * band_rows
        queries = absorb(lax.dynamic_slice_in_dim(query_nope[1], first_row, band_rows, 0), lax.dynamic_slice_in_dim(query_rope[1], first_row, band_rows, 0), up_key)
        prompt = owner_request_table[request_index] // GROUPS
        prompt_low = starts[prompt]
        prompt_high = prompt_ends[prompt]
        fresh_rows = lax.dynamic_slice_in_dim(latent[1], first_row, band_rows, 0)
        step_row = jnp.arange(band_rows, dtype=jnp.int32) // SAMPLES
        sample_row = jnp.arange(band_rows, dtype=jnp.int32) % SAMPLES
        new_visible = (step_row[None, :] <= step_row[:, None]) & (sample_row[None, :] == sample_row[:, None])

        def windowed(window):

            def run_window(unused):
                window_start = jnp.clip(prompt_low, 0, TOKENS - window).astype(jnp.int32)
                cache_keys = lax.dynamic_slice_in_dim(stored, window_start, window, 0)
                cache_scales = lax.dynamic_slice_in_dim(key_scale, window_start, window, 0)
                key_spots = window_start + jnp.arange(window, dtype=jnp.int32)
                old_visible = (key_spots >= prompt_low) & (key_spots < prompt_high)
                key_rows = jnp.concatenate([cache_keys, fresh_rows], axis=0)
                scales = jnp.concatenate([cache_scales, jnp.ones((band_rows,), jnp.bfloat16)], axis=0)
                visible = jnp.concatenate([jnp.broadcast_to(old_visible[None, :], (band_rows, window)), new_visible], axis=1)
                return attend(queries, key_rows, scales, jnp.repeat(visible, HEADS, axis=0))
            return run_window
        latent_result = lax.cond(prompt_high - prompt_low <= short_window, windowed(short_window), windowed(LEN_MOST), 0)
        return project(latent_result, value_up_weight, band_rows)
    prefill_out = lax.map(prefill_block, jnp.arange(N_SEQ, dtype=jnp.int32)).reshape(TOKENS, HEADS, V_DIM)
    decode_out = lax.map(decode_request, jnp.arange(REQUESTS, dtype=jnp.int32)).reshape(TOKENS, HEADS, V_DIM)
    return jnp.stack([prefill_out, decode_out])
```

```python
import functools
import math

import jax
import jax.numpy as jnp
from jax import lax
from jax.experimental import pallas as pl
from jax.experimental.pallas import tpu as pltpu
from jax.sharding import PartitionSpec as P

SAMPLES = 8
STEPS = 4
BLOCK = 64
KEY_TILE = 256
ALIGN = 16
LANES = 128

scale_top = 448.0
tiny_eps = 1e-06
masked_low = -1e30


def absorb_kernel(nope_ref, rope_ref, up_ref, *rest):
    out_ref, wide = rest[-2:]
    tokens, heads, nope_dim = nope_ref.shape
    rank = up_ref.shape[1]
    rope_dim = rope_ref.shape[1] // heads
    wide[...] = nope_ref[...].astype(jnp.float32).reshape(tokens * heads, nope_dim)
    for head in range(heads):
        rows = wide[pl.ds(head, tokens, stride=heads), :].astype(jnp.bfloat16)
        lifted = lax.dot_general(
            rows, up_ref[head], (((1,), (1,)), ((), ())), preferred_element_type=jnp.float32
        )
        out_ref[head, :, :rank] = lifted.astype(jnp.bfloat16)
        rope = rope_ref[:, head * rope_dim : (head + 1) * rope_dim]
        out_ref[head, :, rank : rank + rope_dim] = rope


def absorb(query_nope, query_rope, up_key, group, first, count, prior=None):
    tokens, heads, nope_dim = query_nope.shape
    rank = up_key.shape[1]
    rope_dim = query_rope.shape[1] // heads
    at = first // group
    operands = [
        pltpu.with_memory_space_constraint(operand, pltpu.HBM)
        for operand in (query_nope, query_rope, up_key)
    ]
    in_specs = [
        pl.BlockSpec((tokens, group, nope_dim), lambda g: (0, g + at, 0)),
        pl.BlockSpec((tokens, group * rope_dim), lambda g: (0, g + at)),
        pl.BlockSpec((group, rank, nope_dim), lambda g: (g + at, 0, 0)),
    ]
    if prior is not None:
        in_specs.append(pl.BlockSpec(memory_space=pl.ANY))
        operands.append(prior)
    return pl.pallas_call(
        absorb_kernel,
        grid=(count // group,),
        in_specs=in_specs,
        out_specs=pl.BlockSpec((group, tokens, rank + rope_dim), lambda g: (g + at, 0, 0)),
        out_shape=jax.ShapeDtypeStruct((heads, tokens, rank + rope_dim), jnp.bfloat16),
        scratch_shapes=[pltpu.VMEM((tokens * group, nope_dim), jnp.float32)],
        input_output_aliases={} if prior is None else {3: 0},
        compiler_params=pltpu.CompilerParams(vmem_limit_bytes=16 << 20),
        cost_estimate=pl.CostEstimate(
            flops=2 * tokens * count * nope_dim * rank,
            bytes_accessed=2 * count * (tokens * (nope_dim + rank + 2 * rope_dim) + rank * nope_dim),
            transcendentals=0,
        ),
        name="absorb",
    )(*operands)


def requantized(rows):
    largest = jnp.max(jnp.abs(rows), axis=0, keepdims=True).astype(jnp.float32)
    largest = jnp.max(largest, axis=1, keepdims=True)
    block_scale = ((largest + tiny_eps) / scale_top).astype(jnp.bfloat16).astype(jnp.float32)
    stored = (rows.astype(jnp.float32) * (1.0 / block_scale)).astype(jnp.bfloat16)
    return (stored.astype(jnp.float32) * block_scale).astype(jnp.bfloat16)


def attend_kernel(sizes, lengths_ref, table_ref, query, value_up_hbm, *rest):
    masks, groups, req_dev, rank, rate, tokens_all, most_keys, group = sizes
    compact = most_keys <= 4 * KEY_TILE
    pieces = rest[: 2 * len(masks)]
    own_ref, other_ref, out_hbm, *scratch = rest[2 * len(masks) :]
    keys, band_keys, band_turned, bias, value_up, latent_out, spread, result_rows = scratch[:8]
    score_even, score_odd, top_even, top_odd, placed, sems = scratch[8:]
    heads, tokens, width = query.shape
    band = tokens // req_dev
    rows = group * band
    units = req_dev * (heads // group)
    section, owner, core = (lax.axis_index(name) for name in ("section", "seq", "head"))
    is_decode = section == 1
    prompts = lengths_ref.shape[0]
    step_bits = SAMPLES.bit_length() - 1

    value_copy = pltpu.make_async_copy(value_up_hbm, value_up, sems.at[0])
    value_copy.start()
    virtual = lax.bitwise_xor(owner, section)
    block_copies = []
    for side in range(2):
        side_core = core if side == 0 else 1 - core
        for piece, piece_masks in enumerate(masks):
            source = pieces[side * len(masks) + piece]
            for part, mask in enumerate(piece_masks):
                spot = lax.bitwise_xor(virtual, mask) * 2 + side_core
                rows_at = pl.ds(pl.multiple_of(spot * BLOCK, BLOCK), BLOCK)
                if compact:
                    keys[rows_at, :] = requantized(source[part * BLOCK : (part + 1) * BLOCK, :])
                else:
                    block_copies.append(
                        pltpu.make_async_copy(
                            source.at[pl.ds(part * BLOCK, BLOCK), :],
                            keys.at[rows_at, :],
                            sems.at[1 + len(block_copies)],
                        )
                    )
    for copy in block_copies:
        copy.start()
    pad = keys.shape[0] - tokens_all
    keys[tokens_all:, :] = jnp.zeros((pad, width), jnp.bfloat16)

    starts = []
    running = jnp.int32(0)
    for prompt in range(prompts):
        starts.append(running)
        running = running + lengths_ref[prompt]

    def seen(slot, spots, lines):
        tiles, base, fresh_at, decode_low, decode_high = (placed[slot * 5 + at] for at in range(5))
        first = owner * tokens + slot * band
        held_spot = spots + base
        row_low = jnp.zeros(spots.shape, jnp.int32)
        for prompt in range(prompts):
            row_low = jnp.where(first + lines >= starts[prompt], starts[prompt], row_low)
        row_low = jnp.where(is_decode, decode_low, row_low)
        row_high = jnp.where(is_decode, decode_high, first + lines + 1)
        cached = (held_spot >= row_low) & (held_spot < row_high)
        fresh = spots - fresh_at
        visible_fresh = (
            (fresh >= 0)
            & (fresh < jnp.where(is_decode, band, 0))
            & (jnp.right_shift(fresh, step_bits) <= jnp.right_shift(lines, step_bits))
            & (jnp.bitwise_and(fresh ^ lines, SAMPLES - 1) == 0)
        )
        return jnp.where(cached | visible_fresh, 0.0, masked_low)

    for slot in range(req_dev):
        prompt_of = table_ref[owner * req_dev + slot] // groups
        decode_low = jnp.int32(0)
        decode_high = jnp.int32(0)
        first = owner * tokens + slot * band
        prefill_low = jnp.int32(0)
        for prompt in range(prompts):
            ending = starts[prompt] + lengths_ref[prompt]
            decode_low = jnp.where(prompt_of == prompt, starts[prompt], decode_low)
            decode_high = jnp.where(prompt_of == prompt, ending, decode_high)
            prefill_low = jnp.where(starts[prompt] <= first, starts[prompt], prefill_low)
        low = jnp.where(is_decode, decode_low, prefill_low)
        high = jnp.where(is_decode, decode_high, first + band)
        base = (low // ALIGN) * ALIGN
        fresh_at = ((high - base + ALIGN - 1) // ALIGN) * ALIGN
        tiles = (fresh_at + jnp.where(is_decode, band, 0) + KEY_TILE - 1) // KEY_TILE
        for at, value in enumerate((tiles, base, fresh_at, decode_low, decode_high)):
            placed[slot * 5 + at] = value
        if compact:
            span = (band, bias.shape[1])
            slot_bias = seen(
                slot,
                lax.broadcasted_iota(jnp.int32, span, 1),
                lax.broadcasted_iota(jnp.int32, span, 0),
            )
            bias[slot] = jnp.concatenate([slot_bias] * (LANES // band), axis=0).T

    for copy in block_copies:
        copy.wait()
    if not compact:

        def rescale(block, carry):
            at = pl.ds(pl.multiple_of(block * BLOCK, BLOCK), BLOCK)
            keys[at, :] = requantized(keys[at, :])
            return carry

        lax.fori_loop(0, tokens_all // BLOCK, rescale, 0)
    for slot in range(req_dev):
        tiles, base, fresh_at = (placed[slot * 5 + at] for at in range(3))
        if compact:
            span = band_keys.shape[1]
            band_keys[slot] = keys[pl.ds(pl.multiple_of(base, ALIGN), span), :]
        else:

            def copy_tile(tile, carry):
                target = pl.multiple_of(tile * KEY_TILE, KEY_TILE)
                source = pl.multiple_of(base + tile * KEY_TILE, ALIGN)
                band_keys[slot, pl.ds(target, KEY_TILE), :] = keys[pl.ds(source, KEY_TILE), :]
                return carry

            lax.fori_loop(0, tiles, copy_tile, 0)

        @pl.when(is_decode)
        def add_fresh():
            share = own_ref.shape[0]
            at = slot * band
            mine = at // share
            part = at % share
            for side, source in ((0, own_ref), (1, other_ref)):

                @pl.when((core == mine) == (side == 0))
                def store():
                    band_keys[slot, pl.ds(pl.multiple_of(fresh_at, ALIGN), band), :] = source[
                        part : part + band, :
                    ]

    if compact:
        for slot in range(req_dev):
            band_turned[slot] = band_keys[slot, :, :rank].T

    def spots_of(unit):
        slot = lax.rem(unit, req_dev)
        first_head = pl.multiple_of((unit // req_dev) * group, group)
        return slot, first_head, pl.multiple_of(slot * band, band)

    def scored(unit, key_tile, bias_tile):
        slot, first_head, offset = spots_of(unit)
        asked = query[pl.ds(first_head, group), pl.ds(offset, band), :].reshape(rows, width)
        score = lax.dot_general(
            key_tile, asked, (((1,), (1,)), ((), ())), preferred_element_type=jnp.float32
        )
        return score + jnp.concatenate([bias_tile] * (rows // LANES), axis=1)

    def keep(unit, added, total):
        slot, first_head, offset = spots_of(unit)
        result = (added * (1.0 / total)).astype(jnp.bfloat16)
        latent_out[pl.ds(first_head, group), pl.ds(offset, band), :] = result.T.reshape(
            group, band, rank
        )

    def score_unit(unit, score_ref, top_ref, span):
        slot = lax.rem(unit, req_dev)
        score = scored(unit, band_keys[slot, :span, :], bias[slot, :span, :])
        score_ref[:span, :] = score
        top_ref[...] = jnp.max(score.reshape(span // 8, 8, rows), axis=0)

    def fold_unit(unit, score_ref, top_ref, span):
        slot = lax.rem(unit, req_dev)
        top = jnp.max(top_ref[...], axis=0, keepdims=True)
        expo = jnp.exp2((score_ref[:span, :] - top) * rate)
        total = jnp.sum(expo, axis=0, keepdims=True)
        added = jnp.dot(
            band_turned[slot, :, :span],
            expo.astype(jnp.bfloat16),
            preferred_element_type=jnp.float32,
        )
        keep(unit, added, total)

    many = spread.shape[0] // tokens
    out_copies = []
    for at in range(0, heads, many):
        here = (slice(None), pl.ds(at, many), slice(None))
        out_copies.append(
            pltpu.make_async_copy(
                result_rows.at[here], out_hbm.at[here], sems.at[1 + len(out_copies)]
            )
        )

    def project(part):
        at = part * many
        for head in range(many):
            spread[pl.ds(head, tokens, stride=many), :] = jnp.dot(
                latent_out[at + head], value_up[at + head], preferred_element_type=jnp.float32
            )
        result_rows[:, at : at + many, :] = (
            spread[...].astype(jnp.bfloat16).reshape(tokens, many, result_rows.shape[2])
        )

    def run(span):
        score_unit(0, score_even, top_even, span)

        def pair(index, carry):
            unit = 2 * index
            score_unit(unit + 1, score_odd, top_odd, span)
            fold_unit(unit, score_even, top_even, span)
            score_unit(unit + 2, score_even, top_even, span)
            fold_unit(unit + 1, score_odd, top_odd, span)
            return carry

        lax.fori_loop(0, units // 2 - 1, pair, 0)
        value_copy.wait()
        score_unit(units - 1, score_odd, top_odd, span)
        fold_unit(units - 2, score_even, top_even, span)
        project(0)
        fold_unit(units - 1, score_odd, top_odd, span)
        out_copies[0].start()
        project(1)
        out_copies[1].start()

    def run_long(unit, carry):
        slot = lax.rem(unit, req_dev)

        def step(tile, state):
            top, total, added = state
            at = pl.ds(pl.multiple_of(tile * KEY_TILE, KEY_TILE), KEY_TILE)
            key_tile = band_keys[slot, at, :]
            area = (KEY_TILE, LANES)
            bias_tile = seen(
                slot,
                lax.broadcasted_iota(jnp.int32, area, 0) + tile * KEY_TILE,
                jnp.bitwise_and(lax.broadcasted_iota(jnp.int32, area, 1), band - 1),
            )
            score = scored(unit, key_tile, bias_tile)
            now = jnp.maximum(top, jnp.max(score, axis=0, keepdims=True))
            shrink = jnp.exp2((top - now) * rate)
            expo = jnp.exp2((score - now) * rate)
            term = jnp.dot(
                key_tile[:, :rank].T, expo.astype(jnp.bfloat16), preferred_element_type=jnp.float32
            )
            total = total * shrink + jnp.sum(expo, axis=0, keepdims=True)
            return (now, total, added * shrink + term)

        state = (
            jnp.full((1, rows), masked_low, jnp.float32),
            jnp.zeros((1, rows), jnp.float32),
            jnp.zeros((rank, rows), jnp.float32),
        )
        top, total, added = lax.fori_loop(0, placed[slot * 5], step, state)
        keep(unit, added, total)
        return carry

    if compact:
        tiles = placed[0]
        for slot in range(1, req_dev):
            tiles = jnp.maximum(tiles, placed[slot * 5])
        for count in range(1, -(-most_keys // KEY_TILE) + 1):
            span = min(count * KEY_TILE, most_keys)
            pl.when(tiles == count)(functools.partial(run, span))
    else:
        lax.fori_loop(0, units, run_long, 0)
        value_copy.wait()
        for part, copy in enumerate(out_copies):
            project(part)
            copy.start()
    for copy in out_copies:
        copy.wait()


def attend(
    lengths, table, queries, value_up, pieces, masks, own, other, tokens_all, nope_dim
):
    heads, tokens, width = queries.shape
    rank, v_dim = value_up.shape[1:]
    owners = tokens_all // tokens
    req_dev = table.shape[0] // owners
    groups = table.shape[0] // lengths.shape[0]
    band = tokens // req_dev
    longest = tokens_all // 2 + tokens
    most_keys = -(-(longest + ALIGN + band) // BLOCK) * BLOCK
    room = -(-most_keys // KEY_TILE) * KEY_TILE
    compact = most_keys <= 4 * KEY_TILE
    rate = math.log2(math.e) / math.sqrt(nope_dim + width - rank)
    group = 16
    many = heads // 2
    rows = group * band
    sizes = (masks, groups, req_dev, rank, rate, tokens_all, most_keys, group)
    small = pl.BlockSpec(memory_space=pltpu.SMEM)
    left = pl.BlockSpec(memory_space=pl.ANY)
    whole = pl.BlockSpec(memory_space=pltpu.VMEM)
    score = pltpu.VMEM((room if compact else KEY_TILE, rows), jnp.float32)
    top = pltpu.VMEM((8, rows), jnp.float32)
    return pl.pallas_call(
        functools.partial(attend_kernel, sizes),
        in_specs=[small] * 2
        + [whole, left]
        + [whole if compact else left] * len(pieces)
        + [whole] * 2,
        out_specs=left,
        out_shape=jax.ShapeDtypeStruct((tokens, heads, v_dim), jnp.bfloat16),
        scratch_shapes=[
            pltpu.VMEM((tokens_all + (room if compact else 4 * KEY_TILE), width), jnp.bfloat16),
            pltpu.VMEM((req_dev, room, width), jnp.bfloat16),
            pltpu.VMEM((req_dev, rank, room if compact else LANES), jnp.bfloat16),
            pltpu.VMEM((req_dev, room if compact else 8, LANES), jnp.float32),
            pltpu.VMEM(value_up.shape, jnp.bfloat16),
            pltpu.VMEM((heads, tokens, rank), jnp.bfloat16),
            pltpu.VMEM((tokens * many, v_dim), jnp.float32),
            pltpu.VMEM((tokens, heads, v_dim), jnp.bfloat16),
            score,
            score,
            top,
            top,
            pltpu.SMEM((5 * req_dev,), jnp.int32),
            pltpu.SemaphoreType.DMA((1 + 2 * owners,)),
        ],
        compiler_params=pltpu.CompilerParams(vmem_limit_bytes=(36 if compact else 59) << 20),
        cost_estimate=pl.CostEstimate(
            flops=4 * heads * tokens * longest * width,
            bytes_accessed=2 * (value_up.size + heads * tokens * (width + v_dim)),
            transcendentals=heads * tokens * longest,
        ),
        name="attend",
    )(
        lengths,
        table,
        queries,
        pltpu.with_memory_space_constraint(value_up, pltpu.HBM),
        *pieces,
        own,
        other,
    )


def copy_kernel(source, target):
    target[...] = source[...]


def in_vmem(array):
    whole = pl.BlockSpec(memory_space=pltpu.VMEM)
    return pl.pallas_call(
        copy_kernel,
        in_specs=[whole],
        out_specs=whole,
        out_shape=jax.ShapeDtypeStruct(array.shape, array.dtype),
        compiler_params=pltpu.CompilerParams(vmem_limit_bytes=2 << 20),
        name="hold",
    )(array)


def gathered(latent, absorb_part):
    owners = lax.axis_size("seq")
    flip = lambda bit: [(owner, owner ^ bit) for owner in range(owners)]
    over = lambda chosen, bit: tuple(mask | bit for mask in chosen)
    swap = [(0, 1), (1, 0)]
    beside = lambda part, arrays, prior: lax.optimization_barrier((arrays, absorb_part(part, prior)))
    handed = lax.ppermute(
        latent, ("section", "seq"), [(owner, owners + (owner ^ 1)) for owner in range(owners)]
    )
    fresh = lax.ppermute(latent, "head", swap)
    handed, fresh, own = lax.optimization_barrier((handed, fresh, in_vmem(latent)))
    held = jnp.where(lax.axis_index("section") == 0, own, handed)
    masks = (0,)
    bit = owners // 2
    while bit > 2:
        received = lax.ppermute(held, "seq", flip(bit))
        held = jnp.concatenate([held, received], axis=0)
        masks = masks + over(masks, bit)
        bit //= 2
    swapped = lax.ppermute(held, "section", swap)
    received = lax.ppermute(held, "seq", flip(2))
    held_other = lax.ppermute(held, "head", swap)
    (received, swapped), queries = beside(0, (received, swapped), None)
    crossed = lax.ppermute(received, "seq", flip(1))
    received_other = lax.ppermute(received, "head", swap)
    swapped_other = lax.ppermute(swapped, "head", swap)
    crossed, queries = beside(1, crossed, queries)
    crossed_other = lax.ppermute(crossed, "head", swap)
    pieces = [held, received, swapped, crossed]
    others = [held_other, received_other, swapped_other, crossed_other]
    later = over(masks, 2)
    return pieces + others, (masks, later, over(masks, 1), over(later, 1)), queries, fresh


def shards(query_nope, query_rope, latent, up_key, value_up_weight, lengths, owner_request_table):
    tokens_all = lax.axis_size("seq") * query_nope.shape[1]
    own = latent[0]
    share = query_nope.shape[2] // 2

    def absorb_part(part, prior):
        return absorb(query_nope[0], query_rope[0], up_key, 8, part * share, share, prior)

    pieces, masks, queries, other = gathered(own, absorb_part)
    attended = attend(
        lengths,
        owner_request_table,
        queries,
        value_up_weight,
        pieces,
        masks,
        own,
        other,
        tokens_all,
        query_nope.shape[3],
    )
    return attended[None]


def solution(mesh):
    in_specs = (
        P("section", "seq", "head", None),
        P("section", "seq", "head"),
        P("section", ("seq", "head"), None),
        P("head", None, None),
        P("head", None, None),
        P(),
        P(),
    )
    out_specs = P("section", "seq", "head", None)
    return jax.shard_map(shards, mesh=mesh, in_specs=in_specs, out_specs=out_specs, check_vma=False)
```

```python
import functools
import math

import jax
import jax.numpy as jnp
from jax import lax
from jax.experimental import pallas as pl
from jax.experimental.pallas import tpu as pltpu
from jax.sharding import PartitionSpec as P

SAMPLES = 8
STEPS = 4
BLOCK = 64
KEY_TILE = 256
ALIGN = 16
LANES = 128

EARLY = ((0, 0), (0, 1), (0, 2), (1, 0))
LATE = ((1, 1), (1, 2), (0, 3), (1, 3))

scale_top = 448.0
tiny_eps = 1e-06
masked_low = -1e30


def absorb_kernel(nope_ref, rope_ref, up_ref, *rest):
    out_ref, wide = rest[-2:]
    tokens, heads, nope_dim = nope_ref.shape
    rank = up_ref.shape[1]
    rope_dim = rope_ref.shape[1] // heads
    wide[...] = nope_ref[...].astype(jnp.float32).reshape(tokens * heads, nope_dim)
    for head in range(heads):
        rows = wide[pl.ds(head, tokens, stride=heads), :].astype(jnp.bfloat16)
        lifted = lax.dot_general(
            rows, up_ref[head], (((1,), (1,)), ((), ())), preferred_element_type=jnp.float32
        )
        out_ref[head, :, :rank] = lifted.astype(jnp.bfloat16)
        rope = rope_ref[:, head * rope_dim : (head + 1) * rope_dim]
        out_ref[head, :, rank : rank + rope_dim] = rope


def absorb(query_nope, query_rope, up_key, group, first, count, prior=None):
    tokens, heads, nope_dim = query_nope.shape
    rank = up_key.shape[1]
    rope_dim = query_rope.shape[1] // heads
    at = first // group
    operands = [
        pltpu.with_memory_space_constraint(operand, pltpu.HBM)
        for operand in (query_nope, query_rope, up_key)
    ]
    in_specs = [
        pl.BlockSpec((tokens, group, nope_dim), lambda g: (0, g + at, 0)),
        pl.BlockSpec((tokens, group * rope_dim), lambda g: (0, g + at)),
        pl.BlockSpec((group, rank, nope_dim), lambda g: (g + at, 0, 0)),
    ]
    if prior is not None:
        in_specs.append(pl.BlockSpec(memory_space=pl.ANY))
        operands.append(prior)
    return pl.pallas_call(
        absorb_kernel,
        grid=(count // group,),
        in_specs=in_specs,
        out_specs=pl.BlockSpec((group, tokens, rank + rope_dim), lambda g: (g + at, 0, 0)),
        out_shape=jax.ShapeDtypeStruct((heads, tokens, rank + rope_dim), jnp.bfloat16),
        scratch_shapes=[pltpu.VMEM((tokens * group, nope_dim), jnp.float32)],
        input_output_aliases={} if prior is None else {3: 0},
        compiler_params=pltpu.CompilerParams(vmem_limit_bytes=16 << 20),
        cost_estimate=pl.CostEstimate(
            flops=2 * tokens * count * nope_dim * rank,
            bytes_accessed=2 * count * (tokens * (nope_dim + rank + 2 * rope_dim) + rank * nope_dim),
            transcendentals=0,
        ),
        name="absorb",
    )(*operands)


def requantized(*parts):
    largest = jnp.full((1, 1), 0.0, jnp.float32)
    for part in parts:
        down = jnp.max(jnp.abs(part), axis=0, keepdims=True).astype(jnp.float32)
        largest = jnp.maximum(largest, jnp.max(down, axis=1, keepdims=True))
    block_scale = ((largest + tiny_eps) / scale_top).astype(jnp.bfloat16).astype(jnp.float32)
    inverse = 1.0 / block_scale
    scaled = []
    for part in parts:
        stored = (part.astype(jnp.float32) * inverse).astype(jnp.bfloat16)
        scaled.append((stored.astype(jnp.float32) * block_scale).astype(jnp.bfloat16))
    return scaled


def packed_rope(rope):
    rows = rope.astype(jnp.float32)
    return jnp.concatenate([rows[at : at + 8, :] for at in range(0, BLOCK, 8)], axis=1)


def scaled_block(source, part, keys, rows_at):
    rank = source.shape[1]
    rope_dim = keys.shape[1] - rank
    blocks = source.shape[0] // (BLOCK + 8)
    packed = source[blocks * BLOCK :, :].astype(jnp.float32)[8 * part : 8 * part + 8, :]
    rope = jnp.concatenate(
        [packed[:, at : at + rope_dim] for at in range(0, rank, rope_dim)], axis=0
    )
    rows = source[part * BLOCK : (part + 1) * BLOCK, :]
    scaled, scaled_rope = requantized(rows, rope)
    keys[rows_at, :rank] = scaled
    keys[rows_at, rank:] = scaled_rope


def place_bands(owner, is_decode, lengths_ref, table_ref, groups, req_dev, tokens, placed):
    band = tokens // req_dev
    prompts = lengths_ref.shape[0]
    starts = []
    running = jnp.int32(0)
    for prompt in range(prompts):
        starts.append(running)
        running = running + lengths_ref[prompt]
    for slot in range(req_dev):
        prompt_of = table_ref[owner * req_dev + slot] // groups
        decode_low = jnp.int32(0)
        decode_high = jnp.int32(0)
        first = owner * tokens + slot * band
        prefill_low = jnp.int32(0)
        for prompt in range(prompts):
            ending = starts[prompt] + lengths_ref[prompt]
            decode_low = jnp.where(prompt_of == prompt, starts[prompt], decode_low)
            decode_high = jnp.where(prompt_of == prompt, ending, decode_high)
            prefill_low = jnp.where(starts[prompt] <= first, starts[prompt], prefill_low)
        low = jnp.where(is_decode, decode_low, prefill_low)
        high = jnp.where(is_decode, decode_high, first + band)
        base = (low // ALIGN) * ALIGN
        fresh_at = ((high - base + ALIGN - 1) // ALIGN) * ALIGN
        tiles = (fresh_at + jnp.where(is_decode, band, 0) + KEY_TILE - 1) // KEY_TILE
        for at, value in enumerate((tiles, base, fresh_at, decode_low, decode_high)):
            placed[slot * 5 + at] = value
    return starts


def seen(slot, spots, lines, starts, placed, owner, is_decode, tokens, band):
    step_bits = SAMPLES.bit_length() - 1
    tiles, base, fresh_at, decode_low, decode_high = (placed[slot * 5 + at] for at in range(5))
    first = owner * tokens + slot * band
    held_spot = spots + base
    row_low = jnp.zeros(spots.shape, jnp.int32)
    for start in starts:
        row_low = jnp.where(first + lines >= start, start, row_low)
    row_low = jnp.where(is_decode, decode_low, row_low)
    row_high = jnp.where(is_decode, decode_high, first + lines + 1)
    cached = (held_spot >= row_low) & (held_spot < row_high)
    fresh = spots - fresh_at
    visible_fresh = (
        (fresh >= 0)
        & (fresh < jnp.where(is_decode, band, 0))
        & (jnp.right_shift(fresh, step_bits) <= jnp.right_shift(lines, step_bits))
        & (jnp.bitwise_and(fresh ^ lines, SAMPLES - 1) == 0)
    )
    return jnp.where(cached | visible_fresh, 0.0, masked_low)


def block_spots(masks, owner, section, core, sides):
    virtual = lax.bitwise_xor(owner, section)
    for side, piece in sides:
        side_core = core if side == 0 else 1 - core
        for part, mask in enumerate(masks[piece]):
            spot = lax.bitwise_xor(virtual, mask) * 2 + side_core
            yield part, pl.ds(pl.multiple_of(spot * BLOCK, BLOCK), BLOCK)


def early_kernel(sizes, lengths_ref, table_ref, *rest):
    masks, groups, req_dev, tokens, tokens_all = sizes
    pieces, (keys, bias, placed) = rest[:-3], rest[-3:]
    band = tokens // req_dev
    section, owner, core = (lax.axis_index(name) for name in ("section", "seq", "head"))
    is_decode = section == 1
    for here, source in zip(EARLY, pieces):
        here = [here]
        for part, rows_at in block_spots(masks, owner, section, core, here):
            scaled_block(source, part, keys, rows_at)
    pad = keys.shape[0] - tokens_all
    keys[tokens_all:, :] = jnp.zeros((pad, keys.shape[1]), jnp.bfloat16)
    starts = place_bands(owner, is_decode, lengths_ref, table_ref, groups, req_dev, tokens, placed)
    span = (band, bias.shape[1])
    for slot in range(req_dev):
        slot_bias = seen(
            slot,
            lax.broadcasted_iota(jnp.int32, span, 1),
            lax.broadcasted_iota(jnp.int32, span, 0),
            starts,
            placed,
            owner,
            is_decode,
            tokens,
            band,
        )
        bias[slot] = jnp.concatenate([slot_bias] * (LANES // band), axis=0).T


def attend_kernel(sizes, lengths_ref, table_ref, query, value_up_hbm, *rest):
    masks, groups, req_dev, rank, rate, tokens_all, most_keys, group = sizes
    compact = most_keys <= 4 * KEY_TILE
    count = len(LATE) + 3 if compact else 2 * len(masks)
    pieces = rest[:count]
    own_ref, other_ref, out_hbm, *scratch = rest[count:]
    keys, band_keys, band_turned, value_up, latent_out, spread, result_rows = scratch[:7]
    score_even, score_odd, top_even, top_odd, placed, sems = scratch[7:]
    heads, tokens, width = query.shape
    band = tokens // req_dev
    rows = group * band
    units = req_dev * (heads // group)
    section, owner, core = (lax.axis_index(name) for name in ("section", "seq", "head"))
    is_decode = section == 1

    value_copy = pltpu.make_async_copy(value_up_hbm, value_up, sems.at[0])
    value_copy.start()
    block_copies = []
    starts = []
    if compact:
        *last, early_keys, bias, placed = pieces
        keys[...] = early_keys[...]
        for here, source in zip(LATE, last):
            here = [here]
            for part, rows_at in block_spots(masks, owner, section, core, here):
                scaled_block(source, part, keys, rows_at)
    else:
        for at, source in enumerate(pieces):
            here = [divmod(at, len(masks))]
            for part, rows_at in block_spots(masks, owner, section, core, here):
                block_copies.append(
                    pltpu.make_async_copy(
                        source.at[pl.ds(part * BLOCK, BLOCK), :],
                        keys.at[rows_at, :],
                        sems.at[1 + len(block_copies)],
                    )
                )
        for copy in block_copies:
            copy.start()
        pad = keys.shape[0] - tokens_all
        keys[tokens_all:, :] = jnp.zeros((pad, width), jnp.bfloat16)
        starts = place_bands(
            owner, is_decode, lengths_ref, table_ref, groups, req_dev, tokens, placed
        )

    for copy in block_copies:
        copy.wait()
    if not compact:

        def rescale(block, carry):
            at = pl.ds(pl.multiple_of(block * BLOCK, BLOCK), BLOCK)
            keys[at, :] = requantized(keys[at, :])[0]
            return carry

        lax.fori_loop(0, tokens_all // BLOCK, rescale, 0)
    for slot in range(req_dev):
        tiles, base, fresh_at = (placed[slot * 5 + at] for at in range(3))
        if compact:
            span = band_keys.shape[1]
            band_keys[slot] = keys[pl.ds(pl.multiple_of(base, ALIGN), span), :]
        else:

            def copy_tile(tile, carry):
                target = pl.multiple_of(tile * KEY_TILE, KEY_TILE)
                source = pl.multiple_of(base + tile * KEY_TILE, ALIGN)
                band_keys[slot, pl.ds(target, KEY_TILE), :] = keys[pl.ds(source, KEY_TILE), :]
                return carry

            lax.fori_loop(0, tiles, copy_tile, 0)

        @pl.when(is_decode)
        def add_fresh():
            share = own_ref.shape[0]
            at = slot * band
            mine = at // share
            part = at % share
            for side, source in ((0, own_ref), (1, other_ref)):

                @pl.when((core == mine) == (side == 0))
                def store():
                    band_keys[slot, pl.ds(pl.multiple_of(fresh_at, ALIGN), band), :] = source[
                        part : part + band, :
                    ]

    if compact:
        for slot in range(req_dev):
            band_turned[slot] = band_keys[slot, :, :rank].T

    def spots_of(unit):
        slot = lax.rem(unit, req_dev)
        first_head = pl.multiple_of((unit // req_dev) * group, group)
        return slot, first_head, pl.multiple_of(slot * band, band)

    def scored(unit, key_tile, bias_tile):
        slot, first_head, offset = spots_of(unit)
        asked = query[pl.ds(first_head, group), pl.ds(offset, band), :].reshape(rows, width)
        score = lax.dot_general(
            key_tile, asked, (((1,), (1,)), ((), ())), preferred_element_type=jnp.float32
        )
        return score + jnp.concatenate([bias_tile] * (rows // LANES), axis=1)

    def keep(unit, added, total):
        slot, first_head, offset = spots_of(unit)
        result = (added * (1.0 / total)).astype(jnp.bfloat16)
        latent_out[pl.ds(first_head, group), pl.ds(offset, band), :] = result.T.reshape(
            group, band, rank
        )

    def score_unit(unit, score_ref, top_ref, span):
        slot = lax.rem(unit, req_dev)
        score = scored(unit, band_keys[slot, :span, :], bias[slot, :span, :])
        score_ref[:span, :] = score
        top_ref[...] = jnp.max(score.reshape(span // 8, 8, rows), axis=0)

    def fold_unit(unit, score_ref, top_ref, span):
        slot = lax.rem(unit, req_dev)
        top = jnp.max(top_ref[...], axis=0, keepdims=True)
        expo = jnp.exp2((score_ref[:span, :] - top) * rate)
        total = jnp.sum(expo, axis=0, keepdims=True)
        added = jnp.dot(
            band_turned[slot, :, :span],
            expo.astype(jnp.bfloat16),
            preferred_element_type=jnp.float32,
        )
        keep(unit, added, total)

    many = spread.shape[0] // tokens
    out_copies = []
    for at in range(0, heads, many):
        here = (slice(None), pl.ds(at, many), slice(None))
        out_copies.append(
            pltpu.make_async_copy(
                result_rows.at[here], out_hbm.at[here], sems.at[1 + len(out_copies)]
            )
        )

    def project(part):
        at = part * many
        for head in range(many):
            spread[pl.ds(head, tokens, stride=many), :] = jnp.dot(
                latent_out[at + head], value_up[at + head], preferred_element_type=jnp.float32
            )
        result_rows[:, at : at + many, :] = (
            spread[...].astype(jnp.bfloat16).reshape(tokens, many, result_rows.shape[2])
        )

    def run(span):
        score_unit(0, score_even, top_even, span)

        def pair(index, carry):
            unit = 2 * index
            score_unit(unit + 1, score_odd, top_odd, span)
            fold_unit(unit, score_even, top_even, span)
            score_unit(unit + 2, score_even, top_even, span)
            fold_unit(unit + 1, score_odd, top_odd, span)
            return carry

        lax.fori_loop(0, units // 2 - 1, pair, 0)
        value_copy.wait()
        score_unit(units - 1, score_odd, top_odd, span)
        fold_unit(units - 2, score_even, top_even, span)
        project(0)
        fold_unit(units - 1, score_odd, top_odd, span)
        out_copies[0].start()
        project(1)
        out_copies[1].start()

    def run_long(unit, carry):
        slot = lax.rem(unit, req_dev)

        def step(tile, state):
            top, total, added = state
            at = pl.ds(pl.multiple_of(tile * KEY_TILE, KEY_TILE), KEY_TILE)
            key_tile = band_keys[slot, at, :]
            area = (KEY_TILE, LANES)
            bias_tile = seen(
                slot,
                lax.broadcasted_iota(jnp.int32, area, 0) + tile * KEY_TILE,
                jnp.bitwise_and(lax.broadcasted_iota(jnp.int32, area, 1), band - 1),
                starts,
                placed,
                owner,
                is_decode,
                tokens,
                band,
            )
            score = scored(unit, key_tile, bias_tile)
            now = jnp.maximum(top, jnp.max(score, axis=0, keepdims=True))
            shrink = jnp.exp2((top - now) * rate)
            expo = jnp.exp2((score - now) * rate)
            term = jnp.dot(
                key_tile[:, :rank].T, expo.astype(jnp.bfloat16), preferred_element_type=jnp.float32
            )
            total = total * shrink + jnp.sum(expo, axis=0, keepdims=True)
            return (now, total, added * shrink + term)

        state = (
            jnp.full((1, rows), masked_low, jnp.float32),
            jnp.zeros((1, rows), jnp.float32),
            jnp.zeros((rank, rows), jnp.float32),
        )
        top, total, added = lax.fori_loop(0, placed[slot * 5], step, state)
        keep(unit, added, total)
        return carry

    if compact:
        tiles = placed[0]
        for slot in range(1, req_dev):
            tiles = jnp.maximum(tiles, placed[slot * 5])
        for count in range(1, -(-most_keys // KEY_TILE) + 1):
            span = min(count * KEY_TILE, most_keys)
            pl.when(tiles == count)(functools.partial(run, span))
    else:
        lax.fori_loop(0, units, run_long, 0)
        value_copy.wait()
        for part, copy in enumerate(out_copies):
            project(part)
            copy.start()
    for copy in out_copies:
        copy.wait()


def key_room(tokens, tokens_all, band):
    longest = tokens_all // 2 + tokens
    most_keys = -(-(longest + ALIGN + band) // BLOCK) * BLOCK
    return most_keys, -(-most_keys // KEY_TILE) * KEY_TILE


def prepare_early(lengths, table, masks, pieces, tokens, tokens_all, width):
    req_dev = table.shape[0] // (tokens_all // tokens)
    groups = table.shape[0] // lengths.shape[0]
    room = key_room(tokens, tokens_all, tokens // req_dev)[1]
    small = pl.BlockSpec(memory_space=pltpu.SMEM)
    whole = pl.BlockSpec(memory_space=pltpu.VMEM)
    return pl.pallas_call(
        functools.partial(early_kernel, (masks, groups, req_dev, tokens, tokens_all)),
        in_specs=[small] * 2 + [whole] * len(pieces),
        out_specs=[whole, whole, small],
        out_shape=[
            jax.ShapeDtypeStruct((tokens_all + room, width), jnp.bfloat16),
            jax.ShapeDtypeStruct((req_dev, room, LANES), jnp.float32),
            jax.ShapeDtypeStruct((5 * req_dev,), jnp.int32),
        ],
        compiler_params=pltpu.CompilerParams(vmem_limit_bytes=12 << 20),
        name="early",
    )(lengths, table, *pieces)


def attend(
    lengths, table, queries, value_up, pieces, masks, own, other, tokens_all, nope_dim
):
    heads, tokens, width = queries.shape
    rank, v_dim = value_up.shape[1:]
    owners = tokens_all // tokens
    req_dev = table.shape[0] // owners
    groups = table.shape[0] // lengths.shape[0]
    band = tokens // req_dev
    longest = tokens_all // 2 + tokens
    most_keys, room = key_room(tokens, tokens_all, band)
    compact = most_keys <= 4 * KEY_TILE
    rate = math.log2(math.e) / math.sqrt(nope_dim + width - rank)
    group = 16
    many = heads // 2
    rows = group * band
    sizes = (masks, groups, req_dev, rank, rate, tokens_all, most_keys, group)
    small = pl.BlockSpec(memory_space=pltpu.SMEM)
    left = pl.BlockSpec(memory_space=pl.ANY)
    whole = pl.BlockSpec(memory_space=pltpu.VMEM)
    score = pltpu.VMEM((room if compact else KEY_TILE, rows), jnp.float32)
    top = pltpu.VMEM((8, rows), jnp.float32)
    piece_specs = [whole] * (len(LATE) + 2) + [small] if compact else [left] * len(pieces)
    return pl.pallas_call(
        functools.partial(attend_kernel, sizes),
        in_specs=[small] * 2 + [whole, left] + piece_specs + [whole] * 2,
        out_specs=left,
        out_shape=jax.ShapeDtypeStruct((tokens, heads, v_dim), jnp.bfloat16),
        scratch_shapes=[
            pltpu.VMEM((tokens_all + (room if compact else 4 * KEY_TILE), width), jnp.bfloat16),
            pltpu.VMEM((req_dev, room, width), jnp.bfloat16),
            pltpu.VMEM((req_dev, rank, room if compact else LANES), jnp.bfloat16),
            pltpu.VMEM(value_up.shape, jnp.bfloat16),
            pltpu.VMEM((heads, tokens, rank), jnp.bfloat16),
            pltpu.VMEM((tokens * many, v_dim), jnp.float32),
            pltpu.VMEM((tokens, heads, v_dim), jnp.bfloat16),
            score,
            score,
            top,
            top,
            pltpu.SMEM((5 * req_dev,), jnp.int32),
            pltpu.SemaphoreType.DMA((1 + 2 * owners,)),
        ],
        compiler_params=pltpu.CompilerParams(vmem_limit_bytes=(36 if compact else 59) << 20),
        cost_estimate=pl.CostEstimate(
            flops=4 * heads * tokens * longest * width,
            bytes_accessed=2 * (value_up.size + heads * tokens * (width + v_dim)),
            transcendentals=heads * tokens * longest,
        ),
        name="attend",
    )(
        lengths,
        table,
        queries,
        pltpu.with_memory_space_constraint(value_up, pltpu.HBM),
        *pieces,
        own,
        other,
    )


def copy_kernel(source, target):
    target[...] = source[...]


def choose_kernel(own, handed, target):
    is_prefill = lax.axis_index("section") == 0
    rank = target.shape[1]

    def keep(source):
        if target.shape == source.shape:
            target[...] = source[...]
        else:
            target[:BLOCK, :] = source[:, :rank]
            target[BLOCK:, :] = packed_rope(source[:, rank:]).astype(jnp.bfloat16)

    pl.when(is_prefill)(functools.partial(keep, own))
    pl.when(jnp.logical_not(is_prefill))(functools.partial(keep, handed))


def join_kernel(first, second, target):
    if first.shape[0] % (BLOCK + 8):
        rows = first.shape[0]
        target[:rows, :] = first[...]
        target[rows:, :] = second[...]
    else:
        rows = first.shape[0] // (BLOCK + 8) * BLOCK
        target[:rows, :] = first[:rows, :]
        target[rows : 2 * rows, :] = second[:rows, :]
        ropes = [source[rows:, :].astype(jnp.float32) for source in (first, second)]
        target[2 * rows :, :] = jnp.concatenate(ropes, axis=0).astype(jnp.bfloat16)


def in_vmem(kernel, shape, *arrays):
    whole = pl.BlockSpec(memory_space=pltpu.VMEM)
    return pl.pallas_call(
        kernel,
        in_specs=[whole] * len(arrays),
        out_specs=whole,
        out_shape=jax.ShapeDtypeStruct(shape, arrays[0].dtype),
        compiler_params=pltpu.CompilerParams(vmem_limit_bytes=8 << 20),
        name="hold",
    )(*arrays)


def gathered(latent, absorb_part, early_part, rank):
    owners = lax.axis_size("seq")
    flip = lambda bit: [(owner, owner ^ bit) for owner in range(owners)]
    over = lambda chosen, bit: tuple(mask | bit for mask in chosen)
    swap = [(0, 1), (1, 0)]
    beside = lambda part, arrays, prior: lax.optimization_barrier((arrays, absorb_part(part, prior)))
    handed = lax.ppermute(
        latent, ("section", "seq"), [(owner, owners + (owner ^ 1)) for owner in range(owners)]
    )
    fresh = lax.ppermute(latent, "head", swap)
    block = latent.shape[0]
    own = in_vmem(copy_kernel, latent.shape, latent)
    handed, fresh, own = lax.optimization_barrier((handed, fresh, own))
    shape = latent.shape if early_part is None else (block + 8, rank)
    held = in_vmem(choose_kernel, shape, own, handed)
    masks = (0,)
    bit = owners // 2
    queries = None
    while bit > 2:
        received = lax.ppermute(held, "seq", flip(bit))
        if queries is None:
            received, queries = beside(0, received, None)
        held = in_vmem(join_kernel, (2 * held.shape[0], held.shape[1]), held, received)
        masks = masks + over(masks, bit)
        bit //= 2
    swapped = lax.ppermute(held, "section", swap)
    received = lax.ppermute(held, "seq", flip(2))
    held_other = lax.ppermute(held, "head", swap)
    (received, swapped), queries = beside(1, (received, swapped), queries)
    crossed = lax.ppermute(received, "seq", flip(1))
    received_other = lax.ppermute(received, "head", swap)
    swapped_other = lax.ppermute(swapped, "head", swap)
    later = over(masks, 2)
    all_masks = (masks, later, over(masks, 1), over(later, 1))
    prepared = ()
    if early_part is not None:
        ready = [held, received, swapped, held_other]
        crossed, prepared = lax.optimization_barrier((crossed, early_part(all_masks, ready)))
    crossed_other = lax.ppermute(crossed, "head", swap)
    if early_part is not None:
        pieces = [received_other, swapped_other, crossed, crossed_other, *prepared]
    else:
        pieces = [held, received, swapped, crossed]
        pieces += [held_other, received_other, swapped_other, crossed_other]
    return pieces, all_masks, queries, fresh


def shards(query_nope, query_rope, latent, up_key, value_up_weight, lengths, owner_request_table):
    tokens_all = lax.axis_size("seq") * query_nope.shape[1]
    own = latent[0]
    share = query_nope.shape[2] // 2

    def absorb_part(part, prior):
        return absorb(query_nope[0], query_rope[0], up_key, 8, part * share, share, prior)

    def early_part(masks, pieces):
        tokens, width = query_nope.shape[1], latent.shape[2]
        return prepare_early(
            lengths, owner_request_table, masks, pieces, tokens, tokens_all, width
        )

    compact = tokens_all <= 16 * BLOCK
    pieces, masks, queries, other = gathered(
        own, absorb_part, early_part if compact else None, up_key.shape[1]
    )
    attended = attend(
        lengths,
        owner_request_table,
        queries,
        value_up_weight,
        pieces,
        masks,
        own,
        other,
        tokens_all,
        query_nope.shape[3],
    )
    return attended[None]


def solution(mesh):
    in_specs = (
        P("section", "seq", "head", None),
        P("section", "seq", "head"),
        P("section", ("seq", "head"), None),
        P("head", None, None),
        P("head", None, None),
        P(),
        P(),
    )
    out_specs = P("section", "seq", "head", None)
    return jax.shard_map(shards, mesh=mesh, in_specs=in_specs, out_specs=out_specs, check_vma=False)
```

```python
import functools
import math

import jax
import jax.numpy as jnp
from jax import lax
from jax.experimental import pallas as pl
from jax.experimental.pallas import tpu as pltpu
from jax.sharding import PartitionSpec as P

SAMPLES = 8
STEPS = 4
BLOCK = 64
KEY_TILE = 256
ALIGN = 16
LANES = 128

EARLY = ((0, 0), (0, 1), (0, 2), (1, 0))
LATE = ((1, 1), (1, 2), (0, 3), (1, 3))

scale_top = 448.0
tiny_eps = 1e-06
masked_low = -1e30


def absorb_kernel(nope_ref, rope_ref, up_ref, *rest):
    out_ref, wide = rest[-2:]
    tokens, heads, nope_dim = nope_ref.shape
    rank = up_ref.shape[1]
    rope_dim = rope_ref.shape[1] // heads
    wide[...] = nope_ref[...].astype(jnp.float32).reshape(tokens * heads, nope_dim)
    for head in range(heads):
        rows = wide[pl.ds(head, tokens, stride=heads), :].astype(jnp.bfloat16)
        lifted = lax.dot_general(
            rows, up_ref[head], (((1,), (1,)), ((), ())), preferred_element_type=jnp.float32
        )
        out_ref[head, :, :rank] = lifted.astype(jnp.bfloat16)
        rope = rope_ref[:, head * rope_dim : (head + 1) * rope_dim]
        out_ref[head, :, rank : rank + rope_dim] = rope


def absorb(query_nope, query_rope, up_key, group, first, count, prior=None):
    tokens, heads, nope_dim = query_nope.shape
    rank = up_key.shape[1]
    rope_dim = query_rope.shape[1] // heads
    at = first // group
    operands = [
        pltpu.with_memory_space_constraint(operand, pltpu.HBM)
        for operand in (query_nope, query_rope, up_key)
    ]
    in_specs = [
        pl.BlockSpec((tokens, group, nope_dim), lambda g: (0, g + at, 0)),
        pl.BlockSpec((tokens, group * rope_dim), lambda g: (0, g + at)),
        pl.BlockSpec((group, rank, nope_dim), lambda g: (g + at, 0, 0)),
    ]
    if prior is not None:
        in_specs.append(pl.BlockSpec(memory_space=pl.ANY))
        operands.append(prior)
    return pl.pallas_call(
        absorb_kernel,
        grid=(count // group,),
        in_specs=in_specs,
        out_specs=pl.BlockSpec((group, tokens, rank + rope_dim), lambda g: (g + at, 0, 0)),
        out_shape=jax.ShapeDtypeStruct((heads, tokens, rank + rope_dim), jnp.bfloat16),
        scratch_shapes=[pltpu.VMEM((tokens * group, nope_dim), jnp.float32)],
        input_output_aliases={} if prior is None else {3: 0},
        compiler_params=pltpu.CompilerParams(vmem_limit_bytes=16 << 20),
        cost_estimate=pl.CostEstimate(
            flops=2 * tokens * count * nope_dim * rank,
            bytes_accessed=2 * count * (tokens * (nope_dim + rank + 2 * rope_dim) + rank * nope_dim),
            transcendentals=0,
        ),
        name="absorb",
    )(*operands)


def requantized(*parts):
    largest = jnp.full((1, 1), 0.0, jnp.float32)
    for part in parts:
        down = jnp.max(jnp.abs(part), axis=0, keepdims=True).astype(jnp.float32)
        largest = jnp.maximum(largest, jnp.max(down, axis=1, keepdims=True))
    block_scale = ((largest + tiny_eps) / scale_top).astype(jnp.bfloat16).astype(jnp.float32)
    inverse = 1.0 / block_scale
    scaled = []
    for part in parts:
        stored = (part.astype(jnp.float32) * inverse).astype(jnp.bfloat16)
        scaled.append((stored.astype(jnp.float32) * block_scale).astype(jnp.bfloat16))
    return scaled


def packed_rope(rope):
    rows = rope.astype(jnp.float32)
    return jnp.concatenate([rows[at : at + 8, :] for at in range(0, BLOCK, 8)], axis=1)


def scaled_block(source, part, keys, rows_at):
    rank = source.shape[1]
    rope_dim = keys.shape[1] - rank
    blocks = source.shape[0] // (BLOCK + 8)
    packed = source[blocks * BLOCK :, :].astype(jnp.float32)[8 * part : 8 * part + 8, :]
    rope = jnp.concatenate(
        [packed[:, at : at + rope_dim] for at in range(0, rank, rope_dim)], axis=0
    )
    rows = source[part * BLOCK : (part + 1) * BLOCK, :]
    scaled, scaled_rope = requantized(rows, rope)
    keys[rows_at, :rank] = scaled
    keys[rows_at, rank:] = scaled_rope


def place_bands(owner, is_decode, lengths_ref, table_ref, groups, req_dev, tokens, placed):
    band = tokens // req_dev
    prompts = lengths_ref.shape[0]
    starts = []
    running = jnp.int32(0)
    for prompt in range(prompts):
        starts.append(running)
        running = running + lengths_ref[prompt]
    for slot in range(req_dev):
        prompt_of = table_ref[owner * req_dev + slot] // groups
        decode_low = jnp.int32(0)
        decode_high = jnp.int32(0)
        first = owner * tokens + slot * band
        prefill_low = jnp.int32(0)
        for prompt in range(prompts):
            ending = starts[prompt] + lengths_ref[prompt]
            decode_low = jnp.where(prompt_of == prompt, starts[prompt], decode_low)
            decode_high = jnp.where(prompt_of == prompt, ending, decode_high)
            prefill_low = jnp.where(starts[prompt] <= first, starts[prompt], prefill_low)
        low = jnp.where(is_decode, decode_low, prefill_low)
        high = jnp.where(is_decode, decode_high, first + band)
        base = (low // ALIGN) * ALIGN
        fresh_at = ((high - base + ALIGN - 1) // ALIGN) * ALIGN
        tiles = (fresh_at + jnp.where(is_decode, band, 0) + KEY_TILE - 1) // KEY_TILE
        for at, value in enumerate((tiles, base, fresh_at, decode_low, decode_high)):
            placed[slot * 5 + at] = value
    return starts


def seen(slot, spots, lines, starts, placed, owner, is_decode, tokens, band):
    step_bits = SAMPLES.bit_length() - 1
    tiles, base, fresh_at, decode_low, decode_high = (placed[slot * 5 + at] for at in range(5))
    first = owner * tokens + slot * band
    held_spot = spots + base
    row_low = jnp.zeros(spots.shape, jnp.int32)
    for start in starts:
        row_low = jnp.where(first + lines >= start, start, row_low)
    row_low = jnp.where(is_decode, decode_low, row_low)
    row_high = jnp.where(is_decode, decode_high, first + lines + 1)
    cached = (held_spot >= row_low) & (held_spot < row_high)
    fresh = spots - fresh_at
    visible_fresh = (
        (fresh >= 0)
        & (fresh < jnp.where(is_decode, band, 0))
        & (jnp.right_shift(fresh, step_bits) <= jnp.right_shift(lines, step_bits))
        & (jnp.bitwise_and(fresh ^ lines, SAMPLES - 1) == 0)
    )
    return jnp.where(cached | visible_fresh, 0.0, masked_low)


def block_spots(masks, owner, section, core, sides):
    virtual = lax.bitwise_xor(owner, section)
    for side, piece in sides:
        side_core = core if side == 0 else 1 - core
        for part, mask in enumerate(masks[piece]):
            spot = lax.bitwise_xor(virtual, mask) * 2 + side_core
            yield part, pl.ds(pl.multiple_of(spot * BLOCK, BLOCK), BLOCK)


def early_kernel(sizes, lengths_ref, table_ref, *rest):
    masks, groups, req_dev, tokens, tokens_all = sizes
    pieces, (keys, bias, placed) = rest[:-3], rest[-3:]
    band = tokens // req_dev
    section, owner, core = (lax.axis_index(name) for name in ("section", "seq", "head"))
    is_decode = section == 1
    for here, source in zip(EARLY, pieces):
        here = [here]
        for part, rows_at in block_spots(masks, owner, section, core, here):
            scaled_block(source, part, keys, rows_at)
    pad = keys.shape[0] - tokens_all
    keys[tokens_all:, :] = jnp.zeros((pad, keys.shape[1]), jnp.bfloat16)
    starts = place_bands(owner, is_decode, lengths_ref, table_ref, groups, req_dev, tokens, placed)
    span = (band, bias.shape[1])
    for slot in range(req_dev):
        slot_bias = seen(
            slot,
            lax.broadcasted_iota(jnp.int32, span, 1),
            lax.broadcasted_iota(jnp.int32, span, 0),
            starts,
            placed,
            owner,
            is_decode,
            tokens,
            band,
        )
        bias[slot] = jnp.concatenate([slot_bias] * (LANES // band), axis=0).T


def attend_kernel(sizes, lengths_ref, table_ref, query, value_up_hbm, *rest):
    masks, groups, req_dev, rank, rate, tokens_all, most_keys, group = sizes
    compact = most_keys <= 4 * KEY_TILE
    count = len(LATE) + 3 if compact else 2 * len(masks)
    pieces = rest[:count]
    own_ref, other_ref, out_hbm, *scratch = rest[count:]
    keys, band_keys, band_turned, value_up, latent_out, spread, result_rows = scratch[:7]
    score_even, score_odd, top_even, top_odd, placed, sems = scratch[7:]
    heads, tokens, width = query.shape
    band = tokens // req_dev
    rows = group * band
    units = req_dev * (heads // group)
    section, owner, core = (lax.axis_index(name) for name in ("section", "seq", "head"))
    is_decode = section == 1

    value_copy = pltpu.make_async_copy(value_up_hbm, value_up, sems.at[0])
    value_copy.start()
    block_copies = []
    starts = []
    if compact:
        *last, early_keys, bias, placed = pieces
        keys[...] = early_keys[...]
        for here, source in zip(LATE, last):
            here = [here]
            for part, rows_at in block_spots(masks, owner, section, core, here):
                scaled_block(source, part, keys, rows_at)
    else:
        for at, source in enumerate(pieces):
            here = [divmod(at, len(masks))]
            for part, rows_at in block_spots(masks, owner, section, core, here):
                block_copies.append(
                    pltpu.make_async_copy(
                        source.at[pl.ds(part * BLOCK, BLOCK), :],
                        keys.at[rows_at, :],
                        sems.at[1 + len(block_copies)],
                    )
                )
        for copy in block_copies:
            copy.start()
        pad = keys.shape[0] - tokens_all
        keys[tokens_all:, :] = jnp.zeros((pad, width), jnp.bfloat16)
        starts = place_bands(
            owner, is_decode, lengths_ref, table_ref, groups, req_dev, tokens, placed
        )

    for copy in block_copies:
        copy.wait()
    if not compact:

        def rescale(block, carry):
            at = pl.ds(pl.multiple_of(block * BLOCK, BLOCK), BLOCK)
            keys[at, :] = requantized(keys[at, :])[0]
            return carry

        lax.fori_loop(0, tokens_all // BLOCK, rescale, 0)
    for slot in range(req_dev):
        tiles, base, fresh_at = (placed[slot * 5 + at] for at in range(3))
        if compact:
            span = band_keys.shape[1]
            band_keys[slot] = keys[pl.ds(pl.multiple_of(base, ALIGN), span), :]
        else:

            def copy_tile(tile, carry):
                target = pl.multiple_of(tile * KEY_TILE, KEY_TILE)
                source = pl.multiple_of(base + tile * KEY_TILE, ALIGN)
                band_keys[slot, pl.ds(target, KEY_TILE), :] = keys[pl.ds(source, KEY_TILE), :]
                return carry

            lax.fori_loop(0, tiles, copy_tile, 0)

        @pl.when(is_decode)
        def add_fresh():
            share = own_ref.shape[0]
            at = slot * band
            mine = at // share
            part = at % share
            for side, source in ((0, own_ref), (1, other_ref)):

                @pl.when((core == mine) == (side == 0))
                def store():
                    band_keys[slot, pl.ds(pl.multiple_of(fresh_at, ALIGN), band), :] = source[
                        part : part + band, :
                    ]

    if compact:
        for slot in range(req_dev):
            band_turned[slot] = band_keys[slot, :, :rank].T

    def spots_of(unit):
        if isinstance(unit, int):
            return unit % req_dev, unit // req_dev * group, unit % req_dev * band
        slot = lax.rem(unit, req_dev)
        first_head = pl.multiple_of((unit // req_dev) * group, group)
        return slot, first_head, pl.multiple_of(slot * band, band)

    def scored(unit, key_tile, bias_tile):
        slot, first_head, offset = spots_of(unit)
        asked = query[pl.ds(first_head, group), pl.ds(offset, band), :].reshape(rows, width)
        score = lax.dot_general(
            key_tile, asked, (((1,), (1,)), ((), ())), preferred_element_type=jnp.float32
        )
        return score + jnp.concatenate([bias_tile] * (rows // LANES), axis=1)

    def keep(unit, added, total):
        slot, first_head, offset = spots_of(unit)
        result = (added * (1.0 / total)).astype(jnp.bfloat16)
        latent_out[pl.ds(first_head, group), pl.ds(offset, band), :] = result.T.reshape(
            group, band, rank
        )

    def score_unit(unit, score_ref, top_ref, span):
        slot = unit % req_dev
        score = scored(unit, band_keys[slot, :span, :], bias[slot, :span, :])
        score_ref[:span, :] = score
        top_ref[...] = jnp.max(score.reshape(span // 8, 8, rows), axis=0)

    def fold_unit(unit, score_ref, top_ref, span):
        slot = unit % req_dev
        top = jnp.max(top_ref[...], axis=0, keepdims=True)
        expo = jnp.exp2((score_ref[:span, :] - top) * rate)
        total = jnp.sum(expo, axis=0, keepdims=True)
        added = jnp.dot(
            band_turned[slot, :, :span],
            expo.astype(jnp.bfloat16),
            preferred_element_type=jnp.float32,
        )
        keep(unit, added, total)

    many = spread.shape[0] // tokens
    out_copies = []
    for at in range(0, heads, many):
        here = (slice(None), pl.ds(at, many), slice(None))
        out_copies.append(
            pltpu.make_async_copy(
                result_rows.at[here], out_hbm.at[here], sems.at[1 + len(out_copies)]
            )
        )

    def project(part):
        at = part * many
        for head in range(many):
            spread[pl.ds(head, tokens, stride=many), :] = jnp.dot(
                latent_out[at + head], value_up[at + head], preferred_element_type=jnp.float32
            )
        result_rows[:, at : at + many, :] = (
            spread[...].astype(jnp.bfloat16).reshape(tokens, many, result_rows.shape[2])
        )

    def run(span):
        score_unit(0, score_even, top_even, span)

        for unit in range(0, units - 2, 2):
            score_unit(unit + 1, score_odd, top_odd, span)
            fold_unit(unit, score_even, top_even, span)
            score_unit(unit + 2, score_even, top_even, span)
            fold_unit(unit + 1, score_odd, top_odd, span)
        value_copy.wait()
        score_unit(units - 1, score_odd, top_odd, span)
        fold_unit(units - 2, score_even, top_even, span)
        project(0)
        fold_unit(units - 1, score_odd, top_odd, span)
        out_copies[0].start()
        project(1)
        out_copies[1].start()

    def run_long(unit, carry):
        slot = lax.rem(unit, req_dev)

        def step(tile, state):
            top, total, added = state
            at = pl.ds(pl.multiple_of(tile * KEY_TILE, KEY_TILE), KEY_TILE)
            key_tile = band_keys[slot, at, :]
            area = (KEY_TILE, LANES)
            bias_tile = seen(
                slot,
                lax.broadcasted_iota(jnp.int32, area, 0) + tile * KEY_TILE,
                jnp.bitwise_and(lax.broadcasted_iota(jnp.int32, area, 1), band - 1),
                starts,
                placed,
                owner,
                is_decode,
                tokens,
                band,
            )
            score = scored(unit, key_tile, bias_tile)
            now = jnp.maximum(top, jnp.max(score, axis=0, keepdims=True))
            shrink = jnp.exp2((top - now) * rate)
            expo = jnp.exp2((score - now) * rate)
            term = jnp.dot(
                key_tile[:, :rank].T, expo.astype(jnp.bfloat16), preferred_element_type=jnp.float32
            )
            total = total * shrink + jnp.sum(expo, axis=0, keepdims=True)
            return (now, total, added * shrink + term)

        state = (
            jnp.full((1, rows), masked_low, jnp.float32),
            jnp.zeros((1, rows), jnp.float32),
            jnp.zeros((rank, rows), jnp.float32),
        )
        top, total, added = lax.fori_loop(0, placed[slot * 5], step, state)
        keep(unit, added, total)
        return carry

    if compact:
        tiles = placed[0]
        for slot in range(1, req_dev):
            tiles = jnp.maximum(tiles, placed[slot * 5])
        for count in range(1, -(-most_keys // KEY_TILE) + 1):
            span = min(count * KEY_TILE, most_keys)
            pl.when(tiles == count)(functools.partial(run, span))
    else:
        lax.fori_loop(0, units, run_long, 0)
        value_copy.wait()
        for part, copy in enumerate(out_copies):
            project(part)
            copy.start()
    for copy in out_copies:
        copy.wait()


def key_room(tokens, tokens_all, band):
    longest = tokens_all // 2 + tokens
    most_keys = -(-(longest + ALIGN + band) // BLOCK) * BLOCK
    return most_keys, -(-most_keys // KEY_TILE) * KEY_TILE


def prepare_early(lengths, table, masks, pieces, tokens, tokens_all, width):
    req_dev = table.shape[0] // (tokens_all // tokens)
    groups = table.shape[0] // lengths.shape[0]
    room = key_room(tokens, tokens_all, tokens // req_dev)[1]
    small = pl.BlockSpec(memory_space=pltpu.SMEM)
    whole = pl.BlockSpec(memory_space=pltpu.VMEM)
    return pl.pallas_call(
        functools.partial(early_kernel, (masks, groups, req_dev, tokens, tokens_all)),
        in_specs=[small] * 2 + [whole] * len(pieces),
        out_specs=[whole, whole, small],
        out_shape=[
            jax.ShapeDtypeStruct((tokens_all + room, width), jnp.bfloat16),
            jax.ShapeDtypeStruct((req_dev, room, LANES), jnp.float32),
            jax.ShapeDtypeStruct((5 * req_dev,), jnp.int32),
        ],
        compiler_params=pltpu.CompilerParams(vmem_limit_bytes=12 << 20),
        name="early",
    )(lengths, table, *pieces)


def attend(
    lengths, table, queries, value_up, pieces, masks, own, other, tokens_all, nope_dim
):
    heads, tokens, width = queries.shape
    rank, v_dim = value_up.shape[1:]
    owners = tokens_all // tokens
    req_dev = table.shape[0] // owners
    groups = table.shape[0] // lengths.shape[0]
    band = tokens // req_dev
    longest = tokens_all // 2 + tokens
    most_keys, room = key_room(tokens, tokens_all, band)
    compact = most_keys <= 4 * KEY_TILE
    rate = math.log2(math.e) / math.sqrt(nope_dim + width - rank)
    group = 16
    many = heads // 2
    rows = group * band
    sizes = (masks, groups, req_dev, rank, rate, tokens_all, most_keys, group)
    small = pl.BlockSpec(memory_space=pltpu.SMEM)
    left = pl.BlockSpec(memory_space=pl.ANY)
    whole = pl.BlockSpec(memory_space=pltpu.VMEM)
    score = pltpu.VMEM((room if compact else KEY_TILE, rows), jnp.float32)
    top = pltpu.VMEM((8, rows), jnp.float32)
    piece_specs = [whole] * (len(LATE) + 2) + [small] if compact else [left] * len(pieces)
    return pl.pallas_call(
        functools.partial(attend_kernel, sizes),
        in_specs=[small] * 2 + [whole, left] + piece_specs + [whole] * 2,
        out_specs=left,
        out_shape=jax.ShapeDtypeStruct((tokens, heads, v_dim), jnp.bfloat16),
        scratch_shapes=[
            pltpu.VMEM((tokens_all + (room if compact else 4 * KEY_TILE), width), jnp.bfloat16),
            pltpu.VMEM((req_dev, room, width), jnp.bfloat16),
            pltpu.VMEM((req_dev, rank, room if compact else LANES), jnp.bfloat16),
            pltpu.VMEM(value_up.shape, jnp.bfloat16),
            pltpu.VMEM((heads, tokens, rank), jnp.bfloat16),
            pltpu.VMEM((tokens * many, v_dim), jnp.float32),
            pltpu.VMEM((tokens, heads, v_dim), jnp.bfloat16),
            score,
            score,
            top,
            top,
            pltpu.SMEM((5 * req_dev,), jnp.int32),
            pltpu.SemaphoreType.DMA((1 + 2 * owners,)),
        ],
        compiler_params=pltpu.CompilerParams(vmem_limit_bytes=(36 if compact else 59) << 20),
        cost_estimate=pl.CostEstimate(
            flops=4 * heads * tokens * longest * width,
            bytes_accessed=2 * (value_up.size + heads * tokens * (width + v_dim)),
            transcendentals=heads * tokens * longest,
        ),
        name="attend",
    )(
        lengths,
        table,
        queries,
        pltpu.with_memory_space_constraint(value_up, pltpu.HBM),
        *pieces,
        own,
        other,
    )


def copy_kernel(source, target):
    target[...] = source[...]


def choose_kernel(own, handed, target):
    is_prefill = lax.axis_index("section") == 0
    rank = target.shape[1]

    def keep(source):
        if target.shape == source.shape:
            target[...] = source[...]
        else:
            target[:BLOCK, :] = source[:, :rank]
            target[BLOCK:, :] = packed_rope(source[:, rank:]).astype(jnp.bfloat16)

    pl.when(is_prefill)(functools.partial(keep, own))
    pl.when(jnp.logical_not(is_prefill))(functools.partial(keep, handed))


def join_kernel(first, second, target):
    if first.shape[0] % (BLOCK + 8):
        rows = first.shape[0]
        target[:rows, :] = first[...]
        target[rows:, :] = second[...]
    else:
        rows = first.shape[0] // (BLOCK + 8) * BLOCK
        target[:rows, :] = first[:rows, :]
        target[rows : 2 * rows, :] = second[:rows, :]
        ropes = [source[rows:, :].astype(jnp.float32) for source in (first, second)]
        target[2 * rows :, :] = jnp.concatenate(ropes, axis=0).astype(jnp.bfloat16)


def in_vmem(kernel, shape, *arrays):
    whole = pl.BlockSpec(memory_space=pltpu.VMEM)
    return pl.pallas_call(
        kernel,
        in_specs=[whole] * len(arrays),
        out_specs=whole,
        out_shape=jax.ShapeDtypeStruct(shape, arrays[0].dtype),
        compiler_params=pltpu.CompilerParams(vmem_limit_bytes=8 << 20),
        name="hold",
    )(*arrays)


def gathered(latent, absorb_part, early_part, rank):
    owners = lax.axis_size("seq")
    flip = lambda bit: [(owner, owner ^ bit) for owner in range(owners)]
    over = lambda chosen, bit: tuple(mask | bit for mask in chosen)
    swap = [(0, 1), (1, 0)]
    beside = lambda part, arrays, prior: lax.optimization_barrier((arrays, absorb_part(part, prior)))
    handed = lax.ppermute(
        latent, ("section", "seq"), [(owner, owners + (owner ^ 1)) for owner in range(owners)]
    )
    fresh = lax.ppermute(latent, "head", swap)
    block = latent.shape[0]
    own = in_vmem(copy_kernel, latent.shape, latent)
    handed, fresh, own = lax.optimization_barrier((handed, fresh, own))
    shape = latent.shape if early_part is None else (block + 8, rank)
    held = in_vmem(choose_kernel, shape, own, handed)
    masks = (0,)
    bit = owners // 2
    queries = None
    while bit > 2:
        received = lax.ppermute(held, "seq", flip(bit))
        if queries is None:
            received, queries = beside(0, received, None)
        held = in_vmem(join_kernel, (2 * held.shape[0], held.shape[1]), held, received)
        masks = masks + over(masks, bit)
        bit //= 2
    received = lax.ppermute(held, "seq", flip(2))
    swapped = lax.ppermute(held, "section", swap)
    held_other = lax.ppermute(held, "head", swap)
    received, queries = beside(1, received, queries)
    crossed = lax.ppermute(received, "seq", flip(1))
    received_other = lax.ppermute(received, "head", swap)
    swapped_other = lax.ppermute(swapped, "head", swap)
    later = over(masks, 2)
    all_masks = (masks, later, over(masks, 1), over(later, 1))
    prepared = ()
    if early_part is not None:
        ready = [held, received, swapped, held_other]
        crossed, prepared = lax.optimization_barrier((crossed, early_part(all_masks, ready)))
    crossed_other = lax.ppermute(crossed, "head", swap)
    if early_part is not None:
        pieces = [received_other, swapped_other, crossed, crossed_other, *prepared]
    else:
        pieces = [held, received, swapped, crossed]
        pieces += [held_other, received_other, swapped_other, crossed_other]
    return pieces, all_masks, queries, fresh


def shards(query_nope, query_rope, latent, up_key, value_up_weight, lengths, owner_request_table):
    tokens_all = lax.axis_size("seq") * query_nope.shape[1]
    own = latent[0]
    share = query_nope.shape[2] // 2

    def absorb_part(part, prior):
        return absorb(query_nope[0], query_rope[0], up_key, 8, part * share, share, prior)

    def early_part(masks, pieces):
        tokens, width = query_nope.shape[1], latent.shape[2]
        return prepare_early(
            lengths, owner_request_table, masks, pieces, tokens, tokens_all, width
        )

    compact = tokens_all <= 16 * BLOCK
    pieces, masks, queries, other = gathered(
        own, absorb_part, early_part if compact else None, up_key.shape[1]
    )
    attended = attend(
        lengths,
        owner_request_table,
        queries,
        value_up_weight,
        pieces,
        masks,
        own,
        other,
        tokens_all,
        query_nope.shape[3],
    )
    return attended[None]


def solution(mesh):
    in_specs = (
        P("section", "seq", "head", None),
        P("section", "seq", "head"),
        P("section", ("seq", "head"), None),
        P("head", None, None),
        P("head", None, None),
        P(),
        P(),
    )
    out_specs = P("section", "seq", "head", None)
    return jax.shard_map(shards, mesh=mesh, in_specs=in_specs, out_specs=out_specs, check_vma=False)
```

```python
import functools
import math

import jax
import jax.numpy as jnp
from jax import lax
from jax.experimental import pallas as pl
from jax.experimental.pallas import tpu as pltpu
from jax.sharding import PartitionSpec as P

SAMPLES = 8
STEPS = 4
BLOCK = 64
KEY_TILE = 256
ALIGN = 16
LANES = 128

EARLY = ((0, 0), (0, 1), (0, 2), (1, 0))
LATE = ((1, 1), (1, 2), (0, 3), (1, 3))

scale_top = 448.0
tiny_eps = 1e-06
masked_low = -1e30


def absorb_kernel(nope_ref, rope_ref, up_ref, *rest):
    out_ref, wide = rest[-2:]
    tokens, heads, nope_dim = nope_ref.shape
    rank = up_ref.shape[1]
    rope_dim = rope_ref.shape[1] // heads
    wide[...] = nope_ref[...].astype(jnp.float32).reshape(tokens * heads, nope_dim)
    for head in range(heads):
        rows = wide[pl.ds(head, tokens, stride=heads), :].astype(jnp.bfloat16)
        lifted = lax.dot_general(
            rows, up_ref[head], (((1,), (1,)), ((), ())), preferred_element_type=jnp.float32
        )
        out_ref[head, :, :rank] = lifted.astype(jnp.bfloat16)
        rope = rope_ref[:, head * rope_dim : (head + 1) * rope_dim]
        out_ref[head, :, rank : rank + rope_dim] = rope


def absorb(query_nope, query_rope, up_key, group, first, count, prior=None):
    tokens, heads, nope_dim = query_nope.shape
    rank = up_key.shape[1]
    rope_dim = query_rope.shape[1] // heads
    at = first // group
    operands = [
        pltpu.with_memory_space_constraint(operand, pltpu.HBM)
        for operand in (query_nope, query_rope, up_key)
    ]
    in_specs = [
        pl.BlockSpec((tokens, group, nope_dim), lambda g: (0, g + at, 0)),
        pl.BlockSpec((tokens, group * rope_dim), lambda g: (0, g + at)),
        pl.BlockSpec((group, rank, nope_dim), lambda g: (g + at, 0, 0)),
    ]
    if prior is not None:
        in_specs.append(pl.BlockSpec(memory_space=pl.ANY))
        operands.append(prior)
    return pl.pallas_call(
        absorb_kernel,
        grid=(count // group,),
        in_specs=in_specs,
        out_specs=pl.BlockSpec((group, tokens, rank + rope_dim), lambda g: (g + at, 0, 0)),
        out_shape=jax.ShapeDtypeStruct((heads, tokens, rank + rope_dim), jnp.bfloat16),
        scratch_shapes=[pltpu.VMEM((tokens * group, nope_dim), jnp.float32)],
        input_output_aliases={} if prior is None else {3: 0},
        compiler_params=pltpu.CompilerParams(vmem_limit_bytes=16 << 20),
        cost_estimate=pl.CostEstimate(
            flops=2 * tokens * count * nope_dim * rank,
            bytes_accessed=2 * count * (tokens * (nope_dim + rank + 2 * rope_dim) + rank * nope_dim),
            transcendentals=0,
        ),
        name="absorb",
    )(*operands)


def requantized(*parts):
    largest = jnp.full((1, 1), 0.0, jnp.float32)
    for part in parts:
        down = jnp.max(jnp.abs(part), axis=0, keepdims=True).astype(jnp.float32)
        largest = jnp.maximum(largest, jnp.max(down, axis=1, keepdims=True))
    block_scale = ((largest + tiny_eps) / scale_top).astype(jnp.bfloat16).astype(jnp.float32)
    inverse = 1.0 / block_scale
    scaled = []
    for part in parts:
        stored = (part.astype(jnp.float32) * inverse).astype(jnp.bfloat16)
        scaled.append((stored.astype(jnp.float32) * block_scale).astype(jnp.bfloat16))
    return scaled


def packed_rope(rope):
    rows = rope.astype(jnp.float32)
    return jnp.concatenate([rows[at : at + 8, :] for at in range(0, BLOCK, 8)], axis=1)


def scaled_block(source, part, keys, rows_at):
    rank = source.shape[1]
    rope_dim = keys.shape[1] - rank
    blocks = source.shape[0] // (BLOCK + 8)
    packed = source[blocks * BLOCK :, :].astype(jnp.float32)[8 * part : 8 * part + 8, :]
    rope = jnp.concatenate(
        [packed[:, at : at + rope_dim] for at in range(0, rank, rope_dim)], axis=0
    )
    rows = source[part * BLOCK : (part + 1) * BLOCK, :]
    scaled, scaled_rope = requantized(rows, rope)
    keys[rows_at, :rank] = scaled
    keys[rows_at, rank:] = scaled_rope


def place_bands(owner, is_decode, lengths_ref, table_ref, groups, req_dev, tokens, placed):
    band = tokens // req_dev
    prompts = lengths_ref.shape[0]
    starts = []
    running = jnp.int32(0)
    for prompt in range(prompts):
        starts.append(running)
        running = running + lengths_ref[prompt]
    for slot in range(req_dev):
        prompt_of = table_ref[owner * req_dev + slot] // groups
        decode_low = jnp.int32(0)
        decode_high = jnp.int32(0)
        first = owner * tokens + slot * band
        prefill_low = jnp.int32(0)
        for prompt in range(prompts):
            ending = starts[prompt] + lengths_ref[prompt]
            decode_low = jnp.where(prompt_of == prompt, starts[prompt], decode_low)
            decode_high = jnp.where(prompt_of == prompt, ending, decode_high)
            prefill_low = jnp.where(starts[prompt] <= first, starts[prompt], prefill_low)
        low = jnp.where(is_decode, decode_low, prefill_low)
        high = jnp.where(is_decode, decode_high, first + band)
        base = (low // ALIGN) * ALIGN
        fresh_at = ((high - base + ALIGN - 1) // ALIGN) * ALIGN
        tiles = (fresh_at + jnp.where(is_decode, band, 0) + KEY_TILE - 1) // KEY_TILE
        for at, value in enumerate((tiles, base, fresh_at, decode_low, decode_high)):
            placed[slot * 5 + at] = value
    return starts


def seen(slot, spots, lines, starts, placed, owner, is_decode, tokens, band):
    step_bits = SAMPLES.bit_length() - 1
    tiles, base, fresh_at, decode_low, decode_high = (placed[slot * 5 + at] for at in range(5))
    first = owner * tokens + slot * band
    held_spot = spots + base
    row_low = jnp.zeros(spots.shape, jnp.int32)
    for start in starts:
        row_low = jnp.where(first + lines >= start, start, row_low)
    row_low = jnp.where(is_decode, decode_low, row_low)
    row_high = jnp.where(is_decode, decode_high, first + lines + 1)
    cached = (held_spot >= row_low) & (held_spot < row_high)
    fresh = spots - fresh_at
    visible_fresh = (
        (fresh >= 0)
        & (fresh < jnp.where(is_decode, band, 0))
        & (jnp.right_shift(fresh, step_bits) <= jnp.right_shift(lines, step_bits))
        & (jnp.bitwise_and(fresh ^ lines, SAMPLES - 1) == 0)
    )
    return jnp.where(cached | visible_fresh, 0.0, masked_low)


def block_spots(masks, owner, section, core, sides):
    virtual = lax.bitwise_xor(owner, section)
    for side, piece in sides:
        side_core = core if side == 0 else 1 - core
        for part, mask in enumerate(masks[piece]):
            spot = lax.bitwise_xor(virtual, mask) * 2 + side_core
            yield part, pl.ds(pl.multiple_of(spot * BLOCK, BLOCK), BLOCK)


def early_kernel(sizes, lengths_ref, table_ref, *rest):
    masks, groups, req_dev, tokens, tokens_all = sizes
    pieces, (keys, bias, placed) = rest[:-3], rest[-3:]
    band = tokens // req_dev
    section, owner, core = (lax.axis_index(name) for name in ("section", "seq", "head"))
    is_decode = section == 1
    for here, source in zip(EARLY, pieces):
        here = [here]
        for part, rows_at in block_spots(masks, owner, section, core, here):
            scaled_block(source, part, keys, rows_at)
    pad = keys.shape[0] - tokens_all
    keys[tokens_all:, :] = jnp.zeros((pad, keys.shape[1]), jnp.bfloat16)
    starts = place_bands(owner, is_decode, lengths_ref, table_ref, groups, req_dev, tokens, placed)
    span = (band, bias.shape[1])
    for slot in range(req_dev):
        slot_bias = seen(
            slot,
            lax.broadcasted_iota(jnp.int32, span, 1),
            lax.broadcasted_iota(jnp.int32, span, 0),
            starts,
            placed,
            owner,
            is_decode,
            tokens,
            band,
        )
        bias[slot] = jnp.concatenate([slot_bias] * (LANES // band), axis=0).T


def attend_kernel(sizes, query, value_up_hbm, *rest):
    masks, groups, req_dev, rank, rate, tokens_all, most_keys, group = sizes
    compact = most_keys <= 4 * KEY_TILE
    count = len(LATE) + 3 if compact else 2 * len(masks) + 2
    pieces = rest[:count]
    own_ref, other_ref, out_hbm, *scratch = rest[count:]
    keys, value_up, latent_out, spread, result_rows = scratch[:5]
    score_even, score_odd, top_even, top_odd, placed, sems = scratch[5:11]
    bands = scratch[11:]
    heads, tokens, width = query.shape
    band = tokens // req_dev
    rows = group * band
    units = req_dev * (heads // group)
    section, owner, core = (lax.axis_index(name) for name in ("section", "seq", "head"))
    is_decode = section == 1

    value_copy = pltpu.make_async_copy(value_up_hbm, value_up, sems.at[0])
    value_copy.start()
    block_copies = []
    starts = []
    if compact:
        *last, early_keys, bias, placed = pieces
        keys[...] = early_keys[...]
        for here, source in zip(LATE, last):
            here = [here]
            for part, rows_at in block_spots(masks, owner, section, core, here):
                scaled_block(source, part, keys, rows_at)
    else:
        *pieces, lengths_ref, table_ref = pieces
        for at, source in enumerate(pieces):
            here = [divmod(at, len(masks))]
            for part, rows_at in block_spots(masks, owner, section, core, here):
                block_copies.append(
                    pltpu.make_async_copy(
                        source.at[pl.ds(part * BLOCK, BLOCK), :],
                        keys.at[rows_at, :],
                        sems.at[1 + len(block_copies)],
                    )
                )
        for copy in block_copies:
            copy.start()
        pad = keys.shape[0] - tokens_all
        keys[tokens_all:, :] = jnp.zeros((pad, width), jnp.bfloat16)
        starts = place_bands(
            owner, is_decode, lengths_ref, table_ref, groups, req_dev, tokens, placed
        )

    for copy in block_copies:
        copy.wait()
    if not compact:

        def rescale(block, carry):
            at = pl.ds(pl.multiple_of(block * BLOCK, BLOCK), BLOCK)
            keys[at, :] = requantized(keys[at, :])[0]
            return carry

        lax.fori_loop(0, tokens_all // BLOCK, rescale, 0)
    def keys_of(slot):
        return bands[slot] if compact else bands[0].at[slot]

    def fresh_rows(slot):
        share = own_ref.shape[0]
        mine, part = divmod(slot * band, share)
        here = slice(part, part + band)
        return jnp.where(core == mine, own_ref[here, :], other_ref[here, :])

    def lay_band(slot, span):
        base, fresh_at = (placed[slot * 5 + at] for at in (1, 2))
        extent = -(-span // LANES) * LANES
        band_keys, band_turned = keys_of(slot), bands[req_dev + slot]
        band_keys[:extent, :] = keys[pl.ds(pl.multiple_of(base, ALIGN), extent), :]
        at = pl.ds(pl.multiple_of(fresh_at, ALIGN), band)
        band_keys[at, :] = jnp.where(is_decode, fresh_rows(slot), band_keys[at, :])
        band_turned[:, :extent] = band_keys[:extent, :rank].T

    if not compact:
        for slot in range(req_dev):
            tiles, base, fresh_at = (placed[slot * 5 + at] for at in range(3))
            band_keys = keys_of(slot)

            def copy_tile(tile, carry):
                target = pl.multiple_of(tile * KEY_TILE, KEY_TILE)
                source = pl.multiple_of(base + tile * KEY_TILE, ALIGN)
                band_keys[pl.ds(target, KEY_TILE), :] = keys[pl.ds(source, KEY_TILE), :]
                return carry

            lax.fori_loop(0, tiles, copy_tile, 0)

            @pl.when(is_decode)
            def add_fresh():
                at = pl.ds(pl.multiple_of(fresh_at, ALIGN), band)
                band_keys[at, :] = fresh_rows(slot)

    def spots_of(unit):
        if isinstance(unit, int):
            return unit % req_dev, unit // req_dev * group, unit % req_dev * band
        slot = lax.rem(unit, req_dev)
        first_head = pl.multiple_of((unit // req_dev) * group, group)
        return slot, first_head, pl.multiple_of(slot * band, band)

    def scored(unit, key_tile, bias_tile):
        slot, first_head, offset = spots_of(unit)
        asked = query[pl.ds(first_head, group), pl.ds(offset, band), :].reshape(rows, width)
        score = lax.dot_general(
            key_tile, asked, (((1,), (1,)), ((), ())), preferred_element_type=jnp.float32
        )
        return score + jnp.concatenate([bias_tile] * (rows // LANES), axis=1)

    def keep(unit, added, total):
        slot, first_head, offset = spots_of(unit)
        result = (added * (1.0 / total)).astype(jnp.bfloat16)
        latent_out[pl.ds(first_head, group), pl.ds(offset, band), :] = result.T.reshape(
            group, band, rank
        )

    def score_unit(unit, score_ref, top_ref, span):
        slot = unit % req_dev
        score = scored(unit, keys_of(slot)[:span, :], bias[slot, :span, :])
        score_ref[:span, :] = score
        top_ref[...] = jnp.max(score.reshape(span // 8, 8, rows), axis=0)

    def fold_unit(unit, score_ref, top_ref, span):
        slot = unit % req_dev
        top = jnp.max(top_ref[...], axis=0, keepdims=True)
        expo = jnp.exp2((score_ref[:span, :] - top) * rate)
        total = jnp.sum(expo, axis=0, keepdims=True)
        added = jnp.dot(
            bands[req_dev + slot][:, :span],
            expo.astype(jnp.bfloat16),
            preferred_element_type=jnp.float32,
        )
        keep(unit, added, total)

    many = spread.shape[0] // tokens
    out_copies = []
    for at in range(0, heads, many):
        here = (slice(None), pl.ds(at, many), slice(None))
        out_copies.append(
            pltpu.make_async_copy(
                result_rows.at[here], out_hbm.at[here], sems.at[1 + len(out_copies)]
            )
        )

    def project(part):
        at = part * many
        for head in range(many):
            spread[pl.ds(head, tokens, stride=many), :] = jnp.dot(
                latent_out[at + head], value_up[at + head], preferred_element_type=jnp.float32
            )
        result_rows[:, at : at + many, :] = (
            spread[...].astype(jnp.bfloat16).reshape(tokens, many, result_rows.shape[2])
        )

    def run(span):
        def score_next(unit, score_ref, top_ref):
            if unit < req_dev:
                lay_band(unit, span)
            score_unit(unit, score_ref, top_ref, span)

        score_next(0, score_even, top_even)
        for unit in range(0, units - 2, 2):
            score_next(unit + 1, score_odd, top_odd)
            fold_unit(unit, score_even, top_even, span)
            score_next(unit + 2, score_even, top_even)
            fold_unit(unit + 1, score_odd, top_odd, span)
        value_copy.wait()
        score_unit(units - 1, score_odd, top_odd, span)
        fold_unit(units - 2, score_even, top_even, span)
        project(0)
        fold_unit(units - 1, score_odd, top_odd, span)
        out_copies[0].start()
        project(1)
        out_copies[1].start()

    def run_long(unit, carry):
        slot = lax.rem(unit, req_dev)

        def step(tile, state):
            top, total, added = state
            at = pl.ds(pl.multiple_of(tile * KEY_TILE, KEY_TILE), KEY_TILE)
            key_tile = keys_of(slot)[at, :]
            area = (KEY_TILE, LANES)
            bias_tile = seen(
                slot,
                lax.broadcasted_iota(jnp.int32, area, 0) + tile * KEY_TILE,
                jnp.bitwise_and(lax.broadcasted_iota(jnp.int32, area, 1), band - 1),
                starts,
                placed,
                owner,
                is_decode,
                tokens,
                band,
            )
            score = scored(unit, key_tile, bias_tile)
            now = jnp.maximum(top, jnp.max(score, axis=0, keepdims=True))
            shrink = jnp.exp2((top - now) * rate)
            expo = jnp.exp2((score - now) * rate)
            term = jnp.dot(
                key_tile[:, :rank].T, expo.astype(jnp.bfloat16), preferred_element_type=jnp.float32
            )
            total = total * shrink + jnp.sum(expo, axis=0, keepdims=True)
            return (now, total, added * shrink + term)

        state = (
            jnp.full((1, rows), masked_low, jnp.float32),
            jnp.zeros((1, rows), jnp.float32),
            jnp.zeros((rank, rows), jnp.float32),
        )
        top, total, added = lax.fori_loop(0, placed[slot * 5], step, state)
        keep(unit, added, total)
        return carry

    if compact:
        tiles = placed[0]
        for slot in range(1, req_dev):
            tiles = jnp.maximum(tiles, placed[slot * 5])
        for count in range(1, -(-most_keys // KEY_TILE) + 1):
            span = min(count * KEY_TILE, most_keys)
            pl.when(tiles == count)(functools.partial(run, span))
    else:
        lax.fori_loop(0, units, run_long, 0)
        value_copy.wait()
        for part, copy in enumerate(out_copies):
            project(part)
            copy.start()
    for copy in out_copies:
        copy.wait()


def key_room(tokens, tokens_all, band):
    longest = tokens_all // 2 + tokens
    most_keys = -(-(longest + ALIGN + band) // BLOCK) * BLOCK
    return most_keys, -(-most_keys // KEY_TILE) * KEY_TILE


def prepare_early(lengths, table, masks, pieces, tokens, tokens_all, width):
    req_dev = table.shape[0] // (tokens_all // tokens)
    groups = table.shape[0] // lengths.shape[0]
    room = key_room(tokens, tokens_all, tokens // req_dev)[1]
    small = pl.BlockSpec(memory_space=pltpu.SMEM)
    whole = pl.BlockSpec(memory_space=pltpu.VMEM)
    return pl.pallas_call(
        functools.partial(early_kernel, (masks, groups, req_dev, tokens, tokens_all)),
        in_specs=[small] * 2 + [whole] * len(pieces),
        out_specs=[whole, whole, small],
        out_shape=[
            jax.ShapeDtypeStruct((tokens_all + room, width), jnp.bfloat16),
            jax.ShapeDtypeStruct((req_dev, room, LANES), jnp.float32),
            jax.ShapeDtypeStruct((5 * req_dev,), jnp.int32),
        ],
        compiler_params=pltpu.CompilerParams(vmem_limit_bytes=12 << 20),
        name="early",
    )(lengths, table, *pieces)


def attend(
    lengths, table, queries, value_up, pieces, masks, own, other, tokens_all, nope_dim
):
    heads, tokens, width = queries.shape
    rank, v_dim = value_up.shape[1:]
    owners = tokens_all // tokens
    req_dev = table.shape[0] // owners
    groups = table.shape[0] // lengths.shape[0]
    band = tokens // req_dev
    longest = tokens_all // 2 + tokens
    most_keys, room = key_room(tokens, tokens_all, band)
    compact = most_keys <= 4 * KEY_TILE
    rate = math.log2(math.e) / math.sqrt(nope_dim + width - rank)
    group = 16
    many = heads // 2
    rows = group * band
    sizes = (masks, groups, req_dev, rank, rate, tokens_all, most_keys, group)
    small = pl.BlockSpec(memory_space=pltpu.SMEM)
    left = pl.BlockSpec(memory_space=pl.ANY)
    whole = pl.BlockSpec(memory_space=pltpu.VMEM)
    score = pltpu.VMEM((room if compact else KEY_TILE, rows), jnp.float32)
    top = pltpu.VMEM((8, rows), jnp.float32)
    if compact:
        bands = [pltpu.VMEM((room, width), jnp.bfloat16)] * req_dev
        bands += [pltpu.VMEM((rank, room), jnp.bfloat16)] * req_dev
    else:
        bands = [pltpu.VMEM((req_dev, room, width), jnp.bfloat16)]
        pieces = [*pieces, lengths, table]
    piece_specs = [whole] * (len(LATE) + 2) + [small] if compact else [left] * (len(pieces) - 2) + [small] * 2
    return pl.pallas_call(
        functools.partial(attend_kernel, sizes),
        in_specs=[whole, left] + piece_specs + [whole] * 2,
        out_specs=left,
        out_shape=jax.ShapeDtypeStruct((tokens, heads, v_dim), jnp.bfloat16),
        scratch_shapes=[
            pltpu.VMEM((tokens_all + (room if compact else 4 * KEY_TILE), width), jnp.bfloat16),
            pltpu.VMEM(value_up.shape, jnp.bfloat16),
            pltpu.VMEM((heads, tokens, rank), jnp.bfloat16),
            pltpu.VMEM((tokens * many, v_dim), jnp.float32),
            pltpu.VMEM((tokens, heads, v_dim), jnp.bfloat16),
            score,
            score,
            top,
            top,
            pltpu.SMEM((5 * req_dev,), jnp.int32),
            pltpu.SemaphoreType.DMA((1 + 2 * owners,)),
            *bands,
        ],
        compiler_params=pltpu.CompilerParams(vmem_limit_bytes=(36 if compact else 59) << 20),
        cost_estimate=pl.CostEstimate(
            flops=4 * heads * tokens * longest * width,
            bytes_accessed=2 * (value_up.size + heads * tokens * (width + v_dim)),
            transcendentals=heads * tokens * longest,
        ),
        name="attend",
    )(
        queries,
        pltpu.with_memory_space_constraint(value_up, pltpu.HBM),
        *pieces,
        own,
        other,
    )


def copy_kernel(source, target):
    target[...] = source[...]


def choose_kernel(own, handed, target):
    is_prefill = lax.axis_index("section") == 0
    rank = target.shape[1]

    def keep(source):
        if target.shape == source.shape:
            target[...] = source[...]
        else:
            target[:BLOCK, :] = source[:, :rank]
            target[BLOCK:, :] = packed_rope(source[:, rank:]).astype(jnp.bfloat16)

    pl.when(is_prefill)(functools.partial(keep, own))
    pl.when(jnp.logical_not(is_prefill))(functools.partial(keep, handed))


def join_kernel(first, second, target):
    if first.shape[0] % (BLOCK + 8):
        rows = first.shape[0]
        target[:rows, :] = first[...]
        target[rows:, :] = second[...]
    else:
        rows = first.shape[0] // (BLOCK + 8) * BLOCK
        target[:rows, :] = first[:rows, :]
        target[rows : 2 * rows, :] = second[:rows, :]
        ropes = [source[rows:, :].astype(jnp.float32) for source in (first, second)]
        target[2 * rows :, :] = jnp.concatenate(ropes, axis=0).astype(jnp.bfloat16)


def in_vmem(kernel, shape, *arrays):
    whole = pl.BlockSpec(memory_space=pltpu.VMEM)
    return pl.pallas_call(
        kernel,
        in_specs=[whole] * len(arrays),
        out_specs=whole,
        out_shape=jax.ShapeDtypeStruct(shape, arrays[0].dtype),
        compiler_params=pltpu.CompilerParams(vmem_limit_bytes=8 << 20),
        name="hold",
    )(*arrays)


def gathered(latent, absorb_part, early_part, rank):
    owners = lax.axis_size("seq")
    flip = lambda bit: [(owner, owner ^ bit) for owner in range(owners)]
    over = lambda chosen, bit: tuple(mask | bit for mask in chosen)
    swap = [(0, 1), (1, 0)]
    beside = lambda part, arrays, prior: lax.optimization_barrier((arrays, absorb_part(part, prior)))
    handed = lax.ppermute(
        latent, ("section", "seq"), [(owner, owners + (owner ^ 1)) for owner in range(owners)]
    )
    fresh = lax.ppermute(latent, "head", swap)
    block = latent.shape[0]
    own = in_vmem(copy_kernel, latent.shape, latent)
    handed, fresh, own = lax.optimization_barrier((handed, fresh, own))
    shape = latent.shape if early_part is None else (block + 8, rank)
    held = in_vmem(choose_kernel, shape, own, handed)
    masks = (0,)
    bit = owners // 2
    queries = None
    while bit > 2:
        received = lax.ppermute(held, "seq", flip(bit))
        if queries is None:
            received, queries = beside(0, received, None)
        held = in_vmem(join_kernel, (2 * held.shape[0], held.shape[1]), held, received)
        masks = masks + over(masks, bit)
        bit //= 2
    received = lax.ppermute(held, "seq", flip(2))
    swapped = lax.ppermute(held, "section", swap)
    held_other = lax.ppermute(held, "head", swap)
    received, queries = beside(1, received, queries)
    crossed = lax.ppermute(received, "seq", flip(1))
    received_other = lax.ppermute(received, "head", swap)
    swapped_other = lax.ppermute(swapped, "head", swap)
    later = over(masks, 2)
    all_masks = (masks, later, over(masks, 1), over(later, 1))
    prepared = ()
    if early_part is not None:
        ready = [held, received, swapped, held_other]
        crossed, prepared = lax.optimization_barrier((crossed, early_part(all_masks, ready)))
    crossed_other = lax.ppermute(crossed, "head", swap)
    if early_part is not None:
        pieces = [received_other, swapped_other, crossed, crossed_other, *prepared]
    else:
        pieces = [held, received, swapped, crossed]
        pieces += [held_other, received_other, swapped_other, crossed_other]
    return pieces, all_masks, queries, fresh


def shards(query_nope, query_rope, latent, up_key, value_up_weight, lengths, owner_request_table):
    tokens_all = lax.axis_size("seq") * query_nope.shape[1]
    own = latent[0]
    share = query_nope.shape[2] // 2

    def absorb_part(part, prior):
        return absorb(query_nope[0], query_rope[0], up_key, 8, part * share, share, prior)

    def early_part(masks, pieces):
        tokens, width = query_nope.shape[1], latent.shape[2]
        return prepare_early(
            lengths, owner_request_table, masks, pieces, tokens, tokens_all, width
        )

    compact = tokens_all <= 16 * BLOCK
    pieces, masks, queries, other = gathered(
        own, absorb_part, early_part if compact else None, up_key.shape[1]
    )
    attended = attend(
        lengths,
        owner_request_table,
        queries,
        value_up_weight,
        pieces,
        masks,
        own,
        other,
        tokens_all,
        query_nope.shape[3],
    )
    return attended[None]


def solution(mesh):
    in_specs = (
        P("section", "seq", "head", None),
        P("section", "seq", "head"),
        P("section", ("seq", "head"), None),
        P("head", None, None),
        P("head", None, None),
        P(),
        P(),
    )
    out_specs = P("section", "seq", "head", None)
    return jax.shard_map(shards, mesh=mesh, in_specs=in_specs, out_specs=out_specs, check_vma=False)
```

```python
import functools
import math

import jax
import jax.numpy as jnp
from jax import lax
from jax.experimental import pallas as pl
from jax.experimental.pallas import tpu as pltpu
from jax.sharding import PartitionSpec as P

SAMPLES = 8
STEPS = 4
BLOCK = 64
KEY_TILE = 256
ALIGN = 16
LANES = 128

EARLY = ((0, 0), (0, 1), (0, 2), (1, 0))
LATE = ((1, 1), (1, 2), (0, 3), (1, 3))

scale_top = 448.0
tiny_eps = 1e-06
masked_low = -1e30


def absorb_kernel(nope_ref, rope_ref, up_ref, *rest):
    out_ref, wide = rest[-2:]
    tokens, heads, nope_dim = nope_ref.shape
    rank = up_ref.shape[1]
    rope_dim = rope_ref.shape[1] // heads
    wide[...] = nope_ref[...].astype(jnp.float32).reshape(tokens * heads, nope_dim)
    for head in range(heads):
        rows = wide[pl.ds(head, tokens, stride=heads), :].astype(jnp.bfloat16)
        lifted = lax.dot_general(
            rows, up_ref[head], (((1,), (1,)), ((), ())), preferred_element_type=jnp.float32
        )
        out_ref[head, :, :rank] = lifted.astype(jnp.bfloat16)
        rope = rope_ref[:, head * rope_dim : (head + 1) * rope_dim]
        out_ref[head, :, rank : rank + rope_dim] = rope


def absorb(query_nope, query_rope, up_key, group, first, count, prior=None):
    tokens, heads, nope_dim = query_nope.shape
    rank = up_key.shape[1]
    rope_dim = query_rope.shape[1] // heads
    at = first // group
    operands = [
        pltpu.with_memory_space_constraint(operand, pltpu.HBM)
        for operand in (query_nope, query_rope, up_key)
    ]
    in_specs = [
        pl.BlockSpec((tokens, group, nope_dim), lambda g: (0, g + at, 0)),
        pl.BlockSpec((tokens, group * rope_dim), lambda g: (0, g + at)),
        pl.BlockSpec((group, rank, nope_dim), lambda g: (g + at, 0, 0)),
    ]
    if prior is not None:
        in_specs.append(pl.BlockSpec(memory_space=pl.ANY))
        operands.append(prior)
    return pl.pallas_call(
        absorb_kernel,
        grid=(count // group,),
        in_specs=in_specs,
        out_specs=pl.BlockSpec((group, tokens, rank + rope_dim), lambda g: (g + at, 0, 0)),
        out_shape=jax.ShapeDtypeStruct((heads, tokens, rank + rope_dim), jnp.bfloat16),
        scratch_shapes=[pltpu.VMEM((tokens * group, nope_dim), jnp.float32)],
        input_output_aliases={} if prior is None else {3: 0},
        compiler_params=pltpu.CompilerParams(vmem_limit_bytes=16 << 20),
        cost_estimate=pl.CostEstimate(
            flops=2 * tokens * count * nope_dim * rank,
            bytes_accessed=2 * count * (tokens * (nope_dim + rank + 2 * rope_dim) + rank * nope_dim),
            transcendentals=0,
        ),
        name="absorb",
    )(*operands)


def requantized(*parts):
    largest = jnp.full((1, 1), 0.0, jnp.float32)
    for part in parts:
        down = jnp.max(jnp.abs(part), axis=0, keepdims=True).astype(jnp.float32)
        largest = jnp.maximum(largest, jnp.max(down, axis=1, keepdims=True))
    block_scale = ((largest + tiny_eps) / scale_top).astype(jnp.bfloat16).astype(jnp.float32)
    inverse = 1.0 / block_scale
    scaled = []
    for part in parts:
        stored = (part.astype(jnp.float32) * inverse).astype(jnp.bfloat16)
        scaled.append((stored.astype(jnp.float32) * block_scale).astype(jnp.bfloat16))
    return scaled


def packed_rope(rope):
    rows = rope.astype(jnp.float32)
    return jnp.concatenate([rows[at : at + 8, :] for at in range(0, BLOCK, 8)], axis=1)


def scaled_block(source, part, keys, rows_at):
    rank = source.shape[1]
    rope_dim = keys.shape[1] - rank
    blocks = source.shape[0] // (BLOCK + 8)
    packed = source[blocks * BLOCK :, :].astype(jnp.float32)[8 * part : 8 * part + 8, :]
    rope = jnp.concatenate(
        [packed[:, at : at + rope_dim] for at in range(0, rank, rope_dim)], axis=0
    )
    rows = source[part * BLOCK : (part + 1) * BLOCK, :]
    scaled, scaled_rope = requantized(rows, rope)
    keys[rows_at, :rank] = scaled
    keys[rows_at, rank:] = scaled_rope


def place_bands(owner, is_decode, lengths_ref, table_ref, groups, req_dev, tokens, placed):
    band = tokens // req_dev
    prompts = lengths_ref.shape[0]
    starts = []
    running = jnp.int32(0)
    for prompt in range(prompts):
        starts.append(running)
        running = running + lengths_ref[prompt]
    for slot in range(req_dev):
        prompt_of = table_ref[owner * req_dev + slot] // groups
        decode_low = jnp.int32(0)
        decode_high = jnp.int32(0)
        first = owner * tokens + slot * band
        prefill_low = jnp.int32(0)
        for prompt in range(prompts):
            ending = starts[prompt] + lengths_ref[prompt]
            decode_low = jnp.where(prompt_of == prompt, starts[prompt], decode_low)
            decode_high = jnp.where(prompt_of == prompt, ending, decode_high)
            prefill_low = jnp.where(starts[prompt] <= first, starts[prompt], prefill_low)
        low = jnp.where(is_decode, decode_low, prefill_low)
        high = jnp.where(is_decode, decode_high, first + band)
        base = (low // ALIGN) * ALIGN
        fresh_at = ((high - base + ALIGN - 1) // ALIGN) * ALIGN
        tiles = (fresh_at + jnp.where(is_decode, band, 0) + KEY_TILE - 1) // KEY_TILE
        for at, value in enumerate((tiles, base, fresh_at, decode_low, decode_high)):
            placed[slot * 5 + at] = value
    return starts


def seen(slot, spots, lines, starts, placed, owner, is_decode, tokens, band):
    step_bits = SAMPLES.bit_length() - 1
    tiles, base, fresh_at, decode_low, decode_high = (placed[slot * 5 + at] for at in range(5))
    first = owner * tokens + slot * band
    held_spot = spots + base
    row_low = jnp.zeros(spots.shape, jnp.int32)
    for start in starts:
        row_low = jnp.where(first + lines >= start, start, row_low)
    row_low = jnp.where(is_decode, decode_low, row_low)
    row_high = jnp.where(is_decode, decode_high, first + lines + 1)
    cached = (held_spot >= row_low) & (held_spot < row_high)
    fresh = spots - fresh_at
    visible_fresh = (
        (fresh >= 0)
        & (fresh < jnp.where(is_decode, band, 0))
        & (jnp.right_shift(fresh, step_bits) <= jnp.right_shift(lines, step_bits))
        & (jnp.bitwise_and(fresh ^ lines, SAMPLES - 1) == 0)
    )
    return jnp.where(cached | visible_fresh, 0.0, masked_low)


def block_spots(masks, owner, section, core, sides):
    virtual = lax.bitwise_xor(owner, section)
    for side, piece in sides:
        side_core = core if side == 0 else 1 - core
        for part, mask in enumerate(masks[piece]):
            spot = lax.bitwise_xor(virtual, mask) * 2 + side_core
            yield part, pl.ds(pl.multiple_of(spot * BLOCK, BLOCK), BLOCK)


def early_kernel(sizes, lengths_ref, table_ref, *rest):
    masks, groups, req_dev, tokens, tokens_all = sizes
    pieces, (keys, bias, placed) = rest[:-3], rest[-3:]
    band = tokens // req_dev
    section, owner, core = (lax.axis_index(name) for name in ("section", "seq", "head"))
    is_decode = section == 1
    for here, source in zip(EARLY, pieces):
        here = [here]
        for part, rows_at in block_spots(masks, owner, section, core, here):
            scaled_block(source, part, keys, rows_at)
    pad = keys.shape[0] - tokens_all
    keys[tokens_all:, :] = jnp.zeros((pad, keys.shape[1]), jnp.bfloat16)
    starts = place_bands(owner, is_decode, lengths_ref, table_ref, groups, req_dev, tokens, placed)
    span = (band, bias.shape[1])
    for slot in range(req_dev):
        slot_bias = seen(
            slot,
            lax.broadcasted_iota(jnp.int32, span, 1),
            lax.broadcasted_iota(jnp.int32, span, 0),
            starts,
            placed,
            owner,
            is_decode,
            tokens,
            band,
        )
        bias[slot] = jnp.concatenate([slot_bias] * (LANES // band), axis=0).T


def attend_kernel(sizes, query, value_up_hbm, *rest):
    masks, groups, req_dev, rank, rate, tokens_all, most_keys, group = sizes
    compact = most_keys <= 4 * KEY_TILE
    count = len(LATE) + 3 if compact else 2 * len(masks) + 2
    pieces = rest[:count]
    own_ref, other_ref, out_hbm, *scratch = rest[count:]
    keys, value_up, latent_out, spread, result_rows = scratch[:5]
    score_even, score_odd, top_even, top_odd, placed, sems = scratch[5:11]
    bands = scratch[11:]
    heads, tokens, width = query.shape
    band = tokens // req_dev
    rows = group * band
    units = req_dev * (heads // group)
    section, owner, core = (lax.axis_index(name) for name in ("section", "seq", "head"))
    is_decode = section == 1

    value_copy = pltpu.make_async_copy(value_up_hbm, value_up, sems.at[0])
    value_copy.start()
    block_copies = []
    starts = []
    if compact:
        *last, early_keys, bias, placed = pieces
        keys[...] = early_keys[...]
        for here, source in zip(LATE, last):
            here = [here]
            for part, rows_at in block_spots(masks, owner, section, core, here):
                scaled_block(source, part, keys, rows_at)
    else:
        *pieces, lengths_ref, table_ref = pieces
        for at, source in enumerate(pieces):
            here = [divmod(at, len(masks))]
            for part, rows_at in block_spots(masks, owner, section, core, here):
                block_copies.append(
                    pltpu.make_async_copy(
                        source.at[pl.ds(part * BLOCK, BLOCK), :],
                        keys.at[rows_at, :],
                        sems.at[1 + len(block_copies)],
                    )
                )
        for copy in block_copies:
            copy.start()
        pad = keys.shape[0] - tokens_all
        keys[tokens_all:, :] = jnp.zeros((pad, width), jnp.bfloat16)
        starts = place_bands(
            owner, is_decode, lengths_ref, table_ref, groups, req_dev, tokens, placed
        )

    for copy in block_copies:
        copy.wait()
    if not compact:

        def rescale(block, carry):
            at = pl.ds(pl.multiple_of(block * BLOCK, BLOCK), BLOCK)
            keys[at, :] = requantized(keys[at, :])[0]
            return carry

        lax.fori_loop(0, tokens_all // BLOCK, rescale, 0)
    def keys_of(slot):
        return bands[slot] if compact else bands[0].at[slot]

    def fresh_rows(slot):
        share = own_ref.shape[0]
        mine, part = divmod(slot * band, share)
        here = slice(part, part + band)
        return jnp.where(core == mine, own_ref[here, :], other_ref[here, :])

    def lay_band(slot, span):
        base, fresh_at = (placed[slot * 5 + at] for at in (1, 2))
        extent = -(-span // LANES) * LANES
        band_keys, band_turned = keys_of(slot), bands[req_dev + slot]
        band_keys[:extent, :] = keys[pl.ds(pl.multiple_of(base, ALIGN), extent), :]
        at = pl.ds(pl.multiple_of(fresh_at, ALIGN), band)
        band_keys[at, :] = jnp.where(is_decode, fresh_rows(slot), band_keys[at, :])
        band_turned[:, :extent] = band_keys[:extent, :rank].T

    if not compact:
        for slot in range(req_dev):
            tiles, base, fresh_at = (placed[slot * 5 + at] for at in range(3))
            band_keys = keys_of(slot)

            def copy_tile(tile, carry):
                target = pl.multiple_of(tile * KEY_TILE, KEY_TILE)
                source = pl.multiple_of(base + tile * KEY_TILE, ALIGN)
                band_keys[pl.ds(target, KEY_TILE), :] = keys[pl.ds(source, KEY_TILE), :]
                return carry

            lax.fori_loop(0, tiles, copy_tile, 0)

            @pl.when(is_decode)
            def add_fresh():
                at = pl.ds(pl.multiple_of(fresh_at, ALIGN), band)
                band_keys[at, :] = fresh_rows(slot)

    def spots_of(unit):
        if isinstance(unit, int):
            return unit % req_dev, unit // req_dev * group, unit % req_dev * band
        slot = lax.rem(unit, req_dev)
        first_head = pl.multiple_of((unit // req_dev) * group, group)
        return slot, first_head, pl.multiple_of(slot * band, band)

    def scored(unit, key_tile, bias_tile):
        slot, first_head, offset = spots_of(unit)
        asked = query[pl.ds(first_head, group), pl.ds(offset, band), :].reshape(rows, width)
        score = lax.dot_general(
            key_tile, asked, (((1,), (1,)), ((), ())), preferred_element_type=jnp.float32
        )
        return score + jnp.concatenate([bias_tile] * (rows // LANES), axis=1)

    def keep(unit, added, total):
        slot, first_head, offset = spots_of(unit)
        result = (added * (1.0 / total)).astype(jnp.bfloat16)
        latent_out[pl.ds(first_head, group), pl.ds(offset, band), :] = result.T.reshape(
            group, band, rank
        )

    def score_unit(unit, score_ref, top_ref, span):
        slot = unit % req_dev
        score = scored(unit, keys_of(slot)[:span, :], bias[slot, :span, :])
        score_ref[:span, :] = score
        top_ref[...] = jnp.max(score.reshape(span // 8, 8, rows), axis=0)

    def fold_unit(unit, score_ref, top_ref, span):
        slot = unit % req_dev
        top = jnp.max(top_ref[...], axis=0, keepdims=True)
        expo = jnp.exp2((score_ref[:span, :] - top) * rate)
        total = jnp.sum(expo, axis=0, keepdims=True)
        added = jnp.dot(
            bands[req_dev + slot][:, :span],
            expo.astype(jnp.bfloat16),
            preferred_element_type=jnp.float32,
        )
        keep(unit, added, total)

    many = spread.shape[0] // tokens
    out_copies = []
    for at in range(0, heads, many):
        here = (slice(None), pl.ds(at, many), slice(None))
        out_copies.append(
            pltpu.make_async_copy(
                result_rows.at[here], out_hbm.at[here], sems.at[1 + len(out_copies)]
            )
        )

    def project(part, first=0, last=tokens):
        at = part * many
        for head in range(many):
            spread[pl.ds(first * many + head, last - first, stride=many), :] = jnp.dot(
                latent_out[at + head, first:last, :],
                value_up[at + head],
                preferred_element_type=jnp.float32,
            )
        done = spread[first * many : last * many, :].astype(jnp.bfloat16)
        result_rows[first:last, at : at + many, :] = done.reshape(
            last - first, many, result_rows.shape[2]
        )

    def run(span):
        def score_next(unit, score_ref, top_ref):
            if unit < req_dev:
                lay_band(unit, span)
            score_unit(unit, score_ref, top_ref, span)

        score_next(0, score_even, top_even)
        for unit in range(0, units - 2, 2):
            score_next(unit + 1, score_odd, top_odd)
            fold_unit(unit, score_even, top_even, span)
            if unit == req_dev:
                project(0)
            score_next(unit + 2, score_even, top_even)
            fold_unit(unit + 1, score_odd, top_odd, span)
            if unit == 0:
                value_copy.wait()
        score_unit(units - 1, score_odd, top_odd, span)
        fold_unit(units - 2, score_even, top_even, span)
        project(1, 0, tokens - band)
        fold_unit(units - 1, score_odd, top_odd, span)
        out_copies[0].start()
        project(1, tokens - band, tokens)
        out_copies[1].start()

    def run_long(unit, carry):
        slot = lax.rem(unit, req_dev)

        def step(tile, state):
            top, total, added = state
            at = pl.ds(pl.multiple_of(tile * KEY_TILE, KEY_TILE), KEY_TILE)
            key_tile = keys_of(slot)[at, :]
            area = (KEY_TILE, LANES)
            bias_tile = seen(
                slot,
                lax.broadcasted_iota(jnp.int32, area, 0) + tile * KEY_TILE,
                jnp.bitwise_and(lax.broadcasted_iota(jnp.int32, area, 1), band - 1),
                starts,
                placed,
                owner,
                is_decode,
                tokens,
                band,
            )
            score = scored(unit, key_tile, bias_tile)
            now = jnp.maximum(top, jnp.max(score, axis=0, keepdims=True))
            shrink = jnp.exp2((top - now) * rate)
            expo = jnp.exp2((score - now) * rate)
            term = jnp.dot(
                key_tile[:, :rank].T, expo.astype(jnp.bfloat16), preferred_element_type=jnp.float32
            )
            total = total * shrink + jnp.sum(expo, axis=0, keepdims=True)
            return (now, total, added * shrink + term)

        state = (
            jnp.full((1, rows), masked_low, jnp.float32),
            jnp.zeros((1, rows), jnp.float32),
            jnp.zeros((rank, rows), jnp.float32),
        )
        top, total, added = lax.fori_loop(0, placed[slot * 5], step, state)
        keep(unit, added, total)
        return carry

    if compact:
        tiles = placed[0]
        for slot in range(1, req_dev):
            tiles = jnp.maximum(tiles, placed[slot * 5])
        for count in range(1, -(-most_keys // KEY_TILE) + 1):
            span = min(count * KEY_TILE, most_keys)
            pl.when(tiles == count)(functools.partial(run, span))
    else:
        lax.fori_loop(0, units, run_long, 0)
        value_copy.wait()
        for part, copy in enumerate(out_copies):
            project(part)
            copy.start()
    for copy in out_copies:
        copy.wait()


def key_room(tokens, tokens_all, band):
    longest = tokens_all // 2 + tokens
    most_keys = -(-(longest + ALIGN + band) // BLOCK) * BLOCK
    return most_keys, -(-most_keys // KEY_TILE) * KEY_TILE


def prepare_early(lengths, table, masks, pieces, tokens, tokens_all, width):
    req_dev = table.shape[0] // (tokens_all // tokens)
    groups = table.shape[0] // lengths.shape[0]
    room = key_room(tokens, tokens_all, tokens // req_dev)[1]
    small = pl.BlockSpec(memory_space=pltpu.SMEM)
    whole = pl.BlockSpec(memory_space=pltpu.VMEM)
    return pl.pallas_call(
        functools.partial(early_kernel, (masks, groups, req_dev, tokens, tokens_all)),
        in_specs=[small] * 2 + [whole] * len(pieces),
        out_specs=[whole, whole, small],
        out_shape=[
            jax.ShapeDtypeStruct((tokens_all + room, width), jnp.bfloat16),
            jax.ShapeDtypeStruct((req_dev, room, LANES), jnp.float32),
            jax.ShapeDtypeStruct((5 * req_dev,), jnp.int32),
        ],
        compiler_params=pltpu.CompilerParams(vmem_limit_bytes=12 << 20),
        name="early",
    )(lengths, table, *pieces)


def attend(
    lengths, table, queries, value_up, pieces, masks, own, other, tokens_all, nope_dim
):
    heads, tokens, width = queries.shape
    rank, v_dim = value_up.shape[1:]
    owners = tokens_all // tokens
    req_dev = table.shape[0] // owners
    groups = table.shape[0] // lengths.shape[0]
    band = tokens // req_dev
    longest = tokens_all // 2 + tokens
    most_keys, room = key_room(tokens, tokens_all, band)
    compact = most_keys <= 4 * KEY_TILE
    rate = math.log2(math.e) / math.sqrt(nope_dim + width - rank)
    group = 16
    many = heads // 2
    rows = group * band
    sizes = (masks, groups, req_dev, rank, rate, tokens_all, most_keys, group)
    small = pl.BlockSpec(memory_space=pltpu.SMEM)
    left = pl.BlockSpec(memory_space=pl.ANY)
    whole = pl.BlockSpec(memory_space=pltpu.VMEM)
    score = pltpu.VMEM((room if compact else KEY_TILE, rows), jnp.float32)
    top = pltpu.VMEM((8, rows), jnp.float32)
    if compact:
        bands = [pltpu.VMEM((room, width), jnp.bfloat16)] * req_dev
        bands += [pltpu.VMEM((rank, room), jnp.bfloat16)] * req_dev
    else:
        bands = [pltpu.VMEM((req_dev, room, width), jnp.bfloat16)]
        pieces = [*pieces, lengths, table]
    piece_specs = [whole] * (len(LATE) + 2) + [small] if compact else [left] * (len(pieces) - 2) + [small] * 2
    return pl.pallas_call(
        functools.partial(attend_kernel, sizes),
        in_specs=[whole, left] + piece_specs + [whole] * 2,
        out_specs=left,
        out_shape=jax.ShapeDtypeStruct((tokens, heads, v_dim), jnp.bfloat16),
        scratch_shapes=[
            pltpu.VMEM((tokens_all + (room if compact else 4 * KEY_TILE), width), jnp.bfloat16),
            pltpu.VMEM(value_up.shape, jnp.bfloat16),
            pltpu.VMEM((heads, tokens, rank), jnp.bfloat16),
            pltpu.VMEM((tokens * many, v_dim), jnp.float32),
            pltpu.VMEM((tokens, heads, v_dim), jnp.bfloat16),
            score,
            score,
            top,
            top,
            pltpu.SMEM((5 * req_dev,), jnp.int32),
            pltpu.SemaphoreType.DMA((1 + 2 * owners,)),
            *bands,
        ],
        compiler_params=pltpu.CompilerParams(vmem_limit_bytes=(36 if compact else 59) << 20),
        cost_estimate=pl.CostEstimate(
            flops=4 * heads * tokens * longest * width,
            bytes_accessed=2 * (value_up.size + heads * tokens * (width + v_dim)),
            transcendentals=heads * tokens * longest,
        ),
        name="attend",
    )(
        queries,
        pltpu.with_memory_space_constraint(value_up, pltpu.HBM),
        *pieces,
        own,
        other,
    )


def copy_kernel(source, target):
    target[...] = source[...]


def choose_kernel(own, handed, target):
    is_prefill = lax.axis_index("section") == 0
    rank = target.shape[1]

    def keep(source):
        if target.shape == source.shape:
            target[...] = source[...]
        else:
            target[:BLOCK, :] = source[:, :rank]
            target[BLOCK:, :] = packed_rope(source[:, rank:]).astype(jnp.bfloat16)

    pl.when(is_prefill)(functools.partial(keep, own))
    pl.when(jnp.logical_not(is_prefill))(functools.partial(keep, handed))


def join_kernel(first, second, target):
    if first.shape[0] % (BLOCK + 8):
        rows = first.shape[0]
        target[:rows, :] = first[...]
        target[rows:, :] = second[...]
    else:
        rows = first.shape[0] // (BLOCK + 8) * BLOCK
        target[:rows, :] = first[:rows, :]
        target[rows : 2 * rows, :] = second[:rows, :]
        ropes = [source[rows:, :].astype(jnp.float32) for source in (first, second)]
        target[2 * rows :, :] = jnp.concatenate(ropes, axis=0).astype(jnp.bfloat16)


def in_vmem(kernel, shape, *arrays):
    whole = pl.BlockSpec(memory_space=pltpu.VMEM)
    return pl.pallas_call(
        kernel,
        in_specs=[whole] * len(arrays),
        out_specs=whole,
        out_shape=jax.ShapeDtypeStruct(shape, arrays[0].dtype),
        compiler_params=pltpu.CompilerParams(vmem_limit_bytes=8 << 20),
        name="hold",
    )(*arrays)


def gathered(latent, absorb_part, early_part, rank):
    owners = lax.axis_size("seq")
    flip = lambda bit: [(owner, owner ^ bit) for owner in range(owners)]
    over = lambda chosen, bit: tuple(mask | bit for mask in chosen)
    swap = [(0, 1), (1, 0)]
    beside = lambda part, arrays, prior: lax.optimization_barrier((arrays, absorb_part(part, prior)))
    handed = lax.ppermute(
        latent, ("section", "seq"), [(owner, owners + (owner ^ 1)) for owner in range(owners)]
    )
    fresh = lax.ppermute(latent, "head", swap)
    block = latent.shape[0]
    own = in_vmem(copy_kernel, latent.shape, latent)
    handed, fresh, own = lax.optimization_barrier((handed, fresh, own))
    shape = latent.shape if early_part is None else (block + 8, rank)
    held = in_vmem(choose_kernel, shape, own, handed)
    masks = (0,)
    bit = owners // 2
    queries = None
    while bit > 2:
        received = lax.ppermute(held, "seq", flip(bit))
        if queries is None:
            received, queries = beside(0, received, None)
        held = in_vmem(join_kernel, (2 * held.shape[0], held.shape[1]), held, received)
        masks = masks + over(masks, bit)
        bit //= 2
    received = lax.ppermute(held, "seq", flip(2))
    swapped = lax.ppermute(held, "section", swap)
    held_other = lax.ppermute(held, "head", swap)
    received, queries = beside(1, received, queries)
    crossed = lax.ppermute(received, "seq", flip(1))
    received_other = lax.ppermute(received, "head", swap)
    swapped_other = lax.ppermute(swapped, "head", swap)
    later = over(masks, 2)
    all_masks = (masks, later, over(masks, 1), over(later, 1))
    prepared = ()
    if early_part is not None:
        ready = [held, received, swapped, held_other]
        crossed, prepared = lax.optimization_barrier((crossed, early_part(all_masks, ready)))
    crossed_other = lax.ppermute(crossed, "head", swap)
    if early_part is not None:
        pieces = [received_other, swapped_other, crossed, crossed_other, *prepared]
    else:
        pieces = [held, received, swapped, crossed]
        pieces += [held_other, received_other, swapped_other, crossed_other]
    return pieces, all_masks, queries, fresh


def shards(query_nope, query_rope, latent, up_key, value_up_weight, lengths, owner_request_table):
    tokens_all = lax.axis_size("seq") * query_nope.shape[1]
    own = latent[0]
    share = query_nope.shape[2] // 2

    def absorb_part(part, prior):
        return absorb(query_nope[0], query_rope[0], up_key, 8, part * share, share, prior)

    def early_part(masks, pieces):
        tokens, width = query_nope.shape[1], latent.shape[2]
        return prepare_early(
            lengths, owner_request_table, masks, pieces, tokens, tokens_all, width
        )

    compact = tokens_all <= 16 * BLOCK
    pieces, masks, queries, other = gathered(
        own, absorb_part, early_part if compact else None, up_key.shape[1]
    )
    attended = attend(
        lengths,
        owner_request_table,
        queries,
        value_up_weight,
        pieces,
        masks,
        own,
        other,
        tokens_all,
        query_nope.shape[3],
    )
    return attended[None]


def solution(mesh):
    in_specs = (
        P("section", "seq", "head", None),
        P("section", "seq", "head"),
        P("section", ("seq", "head"), None),
        P("head", None, None),
        P("head", None, None),
        P(),
        P(),
    )
    out_specs = P("section", "seq", "head", None)
    return jax.shard_map(shards, mesh=mesh, in_specs=in_specs, out_specs=out_specs, check_vma=False)
```

```python
import functools
import math

import jax
import jax.numpy as jnp
from jax import lax
from jax.experimental import pallas as pl
from jax.experimental.pallas import tpu as pltpu
from jax.sharding import PartitionSpec as P

SAMPLES = 8
STEPS = 4
BLOCK = 64
KEY_TILE = 256
ALIGN = 16
LANES = 128

EARLY = ((0, 0), (0, 1), (0, 2), (1, 0))
LATE = ((1, 1), (1, 2), (0, 3), (1, 3))

scale_top = 448.0
tiny_eps = 1e-06
masked_low = -1e30


def absorb_kernel(carries, nope_ref, rope_ref, up_ref, *rest):
    if carries:
        carried_ref, out_ref, copied_ref, wide = rest
        copied_ref[...] = carried_ref[...]
    else:
        _, out_ref, wide = rest
    tokens, heads, nope_dim = nope_ref.shape
    rank = up_ref.shape[1]
    rope_dim = rope_ref.shape[1] // heads
    wide[...] = nope_ref[...].astype(jnp.float32).reshape(tokens * heads, nope_dim)
    for head in range(heads):
        rows = wide[pl.ds(head, tokens, stride=heads), :].astype(jnp.bfloat16)
        lifted = lax.dot_general(
            rows, up_ref[head], (((1,), (1,)), ((), ())), preferred_element_type=jnp.float32
        )
        out_ref[head, :, :rank] = lifted.astype(jnp.bfloat16)
        rope = rope_ref[:, head * rope_dim : (head + 1) * rope_dim]
        out_ref[head, :, rank : rank + rope_dim] = rope


def absorb(query_nope, query_rope, up_key, group, first, count, carried=None, prior=None):
    tokens, heads, nope_dim = query_nope.shape
    rank = up_key.shape[1]
    rope_dim = query_rope.shape[1] // heads
    at = first // group
    operands = [query_nope, query_rope, up_key]
    in_specs = [
        pl.BlockSpec((tokens, group, nope_dim), lambda g: (0, g + at, 0)),
        pl.BlockSpec((tokens, group * rope_dim), lambda g: (0, g + at)),
        pl.BlockSpec((group, rank, nope_dim), lambda g: (g + at, 0, 0)),
    ]
    out_specs = [pl.BlockSpec((group, tokens, rank + rope_dim), lambda g: (g + at, 0, 0))]
    out_shape = [jax.ShapeDtypeStruct((heads, tokens, rank + rope_dim), jnp.bfloat16)]
    if carried is not None:
        same = pl.BlockSpec(carried.shape, lambda g: (0, 0))
        in_specs.append(same)
        operands.append(carried)
        out_specs.append(same)
        out_shape.append(jax.ShapeDtypeStruct(carried.shape, carried.dtype))
    operands = [pltpu.with_memory_space_constraint(operand, pltpu.HBM) for operand in operands]
    if prior is not None:
        in_specs.append(pl.BlockSpec(memory_space=pl.ANY))
        operands.append(prior)
    return pl.pallas_call(
        functools.partial(absorb_kernel, carried is not None),
        grid=(count // group,),
        in_specs=in_specs,
        out_specs=out_specs,
        out_shape=out_shape,
        scratch_shapes=[pltpu.VMEM((tokens * group, nope_dim), jnp.float32)],
        input_output_aliases={} if prior is None else {3: 0},
        compiler_params=pltpu.CompilerParams(vmem_limit_bytes=16 << 20),
        cost_estimate=pl.CostEstimate(
            flops=2 * tokens * count * nope_dim * rank,
            bytes_accessed=2 * count * (tokens * (nope_dim + rank + 2 * rope_dim) + rank * nope_dim),
            transcendentals=0,
        ),
        name="absorb",
    )(*operands)


def requantized(*parts):
    largest = jnp.full((1, 1), 0.0, jnp.float32)
    for part in parts:
        down = jnp.max(jnp.abs(part), axis=0, keepdims=True).astype(jnp.float32)
        largest = jnp.maximum(largest, jnp.max(down, axis=1, keepdims=True))
    block_scale = ((largest + tiny_eps) / scale_top).astype(jnp.bfloat16).astype(jnp.float32)
    inverse = 1.0 / block_scale
    scaled = []
    for part in parts:
        stored = (part.astype(jnp.float32) * inverse).astype(jnp.bfloat16)
        scaled.append((stored.astype(jnp.float32) * block_scale).astype(jnp.bfloat16))
    return scaled


def packed_rope(rope):
    rows = rope.astype(jnp.float32)
    return jnp.concatenate([rows[at : at + 8, :] for at in range(0, BLOCK, 8)], axis=1)


def scaled_block(source, part, keys, rows_at):
    rank = source.shape[1]
    rope_dim = keys.shape[1] - rank
    blocks = source.shape[0] // (BLOCK + 8)
    packed = source[blocks * BLOCK :, :].astype(jnp.float32)[8 * part : 8 * part + 8, :]
    rope = jnp.concatenate(
        [packed[:, at : at + rope_dim] for at in range(0, rank, rope_dim)], axis=0
    )
    rows = source[part * BLOCK : (part + 1) * BLOCK, :]
    scaled, scaled_rope = requantized(rows, rope)
    keys[rows_at, :rank] = scaled
    keys[rows_at, rank:] = scaled_rope


def place_bands(owner, is_decode, lengths_ref, table_ref, groups, req_dev, tokens, placed):
    band = tokens // req_dev
    prompts = lengths_ref.shape[0]
    starts = []
    running = jnp.int32(0)
    for prompt in range(prompts):
        starts.append(running)
        running = running + lengths_ref[prompt]
    for slot in range(req_dev):
        prompt_of = table_ref[owner * req_dev + slot] // groups
        decode_low = jnp.int32(0)
        decode_high = jnp.int32(0)
        first = owner * tokens + slot * band
        prefill_low = jnp.int32(0)
        for prompt in range(prompts):
            ending = starts[prompt] + lengths_ref[prompt]
            decode_low = jnp.where(prompt_of == prompt, starts[prompt], decode_low)
            decode_high = jnp.where(prompt_of == prompt, ending, decode_high)
            prefill_low = jnp.where(starts[prompt] <= first, starts[prompt], prefill_low)
        low = jnp.where(is_decode, decode_low, prefill_low)
        high = jnp.where(is_decode, decode_high, first + band)
        base = (low // ALIGN) * ALIGN
        fresh_at = ((high - base + ALIGN - 1) // ALIGN) * ALIGN
        tiles = (fresh_at + jnp.where(is_decode, band, 0) + KEY_TILE - 1) // KEY_TILE
        for at, value in enumerate((tiles, base, fresh_at, decode_low, decode_high)):
            placed[slot * 5 + at] = value
    return starts


def seen(slot, spots, lines, starts, placed, owner, is_decode, tokens, band):
    step_bits = SAMPLES.bit_length() - 1
    tiles, base, fresh_at, decode_low, decode_high = (placed[slot * 5 + at] for at in range(5))
    first = owner * tokens + slot * band
    held_spot = spots + base
    row_low = jnp.zeros(spots.shape, jnp.int32)
    for start in starts:
        row_low = jnp.where(first + lines >= start, start, row_low)
    row_low = jnp.where(is_decode, decode_low, row_low)
    row_high = jnp.where(is_decode, decode_high, first + lines + 1)
    cached = (held_spot >= row_low) & (held_spot < row_high)
    fresh = spots - fresh_at
    visible_fresh = (
        (fresh >= 0)
        & (fresh < jnp.where(is_decode, band, 0))
        & (jnp.right_shift(fresh, step_bits) <= jnp.right_shift(lines, step_bits))
        & (jnp.bitwise_and(fresh ^ lines, SAMPLES - 1) == 0)
    )
    return jnp.where(cached | visible_fresh, 0.0, masked_low)


def block_spots(masks, owner, section, core, sides):
    virtual = lax.bitwise_xor(owner, section)
    for side, piece in sides:
        side_core = core if side == 0 else 1 - core
        for part, mask in enumerate(masks[piece]):
            spot = lax.bitwise_xor(virtual, mask) * 2 + side_core
            yield part, pl.ds(pl.multiple_of(spot * BLOCK, BLOCK), BLOCK)


def early_kernel(sizes, lengths_ref, table_ref, *rest):
    masks, groups, req_dev, tokens, tokens_all = sizes
    pieces, (keys, bias, placed) = rest[:-3], rest[-3:]
    band = tokens // req_dev
    section, owner, core = (lax.axis_index(name) for name in ("section", "seq", "head"))
    is_decode = section == 1
    for here, source in zip(EARLY, pieces):
        here = [here]
        for part, rows_at in block_spots(masks, owner, section, core, here):
            scaled_block(source, part, keys, rows_at)
    pad = keys.shape[0] - tokens_all
    keys[tokens_all:, :] = jnp.zeros((pad, keys.shape[1]), jnp.bfloat16)
    starts = place_bands(owner, is_decode, lengths_ref, table_ref, groups, req_dev, tokens, placed)
    span = (band, bias.shape[1])
    for slot in range(req_dev):
        slot_bias = seen(
            slot,
            lax.broadcasted_iota(jnp.int32, span, 1),
            lax.broadcasted_iota(jnp.int32, span, 0),
            starts,
            placed,
            owner,
            is_decode,
            tokens,
            band,
        )
        bias[slot] = jnp.concatenate([slot_bias] * (LANES // band), axis=0).T


def attend_kernel(sizes, query, value_up_hbm, *rest):
    masks, groups, req_dev, rank, rate, tokens_all, most_keys, group = sizes
    compact = most_keys <= 4 * KEY_TILE
    count = len(LATE) + 3 if compact else 2 * len(masks) + 2
    pieces = rest[:count]
    own_ref, other_ref, out_hbm, *scratch = rest[count:]
    keys, value_up, latent_out, spread, result_rows = scratch[:5]
    score_even, score_odd, top_even, top_odd, placed, sems = scratch[5:11]
    bands = scratch[11:]
    heads, tokens, width = query.shape
    band = tokens // req_dev
    rows = group * band
    units = req_dev * (heads // group)
    section, owner, core = (lax.axis_index(name) for name in ("section", "seq", "head"))
    is_decode = section == 1

    value_copy = pltpu.make_async_copy(value_up_hbm, value_up, sems.at[0])
    value_copy.start()
    block_copies = []
    starts = []
    if compact:
        *last, early_keys, bias, placed = pieces
        keys[...] = early_keys[...]
        for here, source in zip(LATE, last):
            here = [here]
            for part, rows_at in block_spots(masks, owner, section, core, here):
                scaled_block(source, part, keys, rows_at)
    else:
        *pieces, lengths_ref, table_ref = pieces
        for at, source in enumerate(pieces):
            here = [divmod(at, len(masks))]
            for part, rows_at in block_spots(masks, owner, section, core, here):
                block_copies.append(
                    pltpu.make_async_copy(
                        source.at[pl.ds(part * BLOCK, BLOCK), :],
                        keys.at[rows_at, :],
                        sems.at[1 + len(block_copies)],
                    )
                )
        for copy in block_copies:
            copy.start()
        pad = keys.shape[0] - tokens_all
        keys[tokens_all:, :] = jnp.zeros((pad, width), jnp.bfloat16)
        starts = place_bands(
            owner, is_decode, lengths_ref, table_ref, groups, req_dev, tokens, placed
        )

    for copy in block_copies:
        copy.wait()
    if not compact:

        def rescale(block, carry):
            at = pl.ds(pl.multiple_of(block * BLOCK, BLOCK), BLOCK)
            keys[at, :] = requantized(keys[at, :])[0]
            return carry

        lax.fori_loop(0, tokens_all // BLOCK, rescale, 0)
    def keys_of(slot):
        return bands[slot] if compact else bands[0].at[slot]

    def fresh_rows(slot):
        share = own_ref.shape[0]
        mine, part = divmod(slot * band, share)
        here = slice(part, part + band)
        return jnp.where(core == mine, own_ref[here, :], other_ref[here, :])

    def lay_band(slot, span):
        base, fresh_at = (placed[slot * 5 + at] for at in (1, 2))
        extent = -(-span // LANES) * LANES
        band_keys, band_turned = keys_of(slot), bands[req_dev + slot]
        band_keys[:extent, :] = keys[pl.ds(pl.multiple_of(base, ALIGN), extent), :]
        at = pl.ds(pl.multiple_of(fresh_at, ALIGN), band)
        band_keys[at, :] = jnp.where(is_decode, fresh_rows(slot), band_keys[at, :])
        band_turned[:, :extent] = band_keys[:extent, :rank].T

    if not compact:
        for slot in range(req_dev):
            tiles, base, fresh_at = (placed[slot * 5 + at] for at in range(3))
            band_keys = keys_of(slot)

            def copy_tile(tile, carry):
                target = pl.multiple_of(tile * KEY_TILE, KEY_TILE)
                source = pl.multiple_of(base + tile * KEY_TILE, ALIGN)
                band_keys[pl.ds(target, KEY_TILE), :] = keys[pl.ds(source, KEY_TILE), :]
                return carry

            lax.fori_loop(0, tiles, copy_tile, 0)

            @pl.when(is_decode)
            def add_fresh():
                at = pl.ds(pl.multiple_of(fresh_at, ALIGN), band)
                band_keys[at, :] = fresh_rows(slot)

    def spots_of(unit):
        if isinstance(unit, int):
            return unit % req_dev, unit // req_dev * group, unit % req_dev * band
        slot = lax.rem(unit, req_dev)
        first_head = pl.multiple_of((unit // req_dev) * group, group)
        return slot, first_head, pl.multiple_of(slot * band, band)

    def scored(unit, key_tile, bias_tile):
        slot, first_head, offset = spots_of(unit)
        asked = query[pl.ds(first_head, group), pl.ds(offset, band), :].reshape(rows, width)
        score = lax.dot_general(
            key_tile, asked, (((1,), (1,)), ((), ())), preferred_element_type=jnp.float32
        )
        return score + jnp.concatenate([bias_tile] * (rows // LANES), axis=1)

    def keep(unit, added, total):
        slot, first_head, offset = spots_of(unit)
        result = (added * (1.0 / total)).astype(jnp.bfloat16)
        latent_out[pl.ds(first_head, group), pl.ds(offset, band), :] = result.T.reshape(
            group, band, rank
        )

    def score_unit(unit, score_ref, top_ref, span):
        slot = unit % req_dev
        score = scored(unit, keys_of(slot)[:span, :], bias[slot, :span, :])
        score_ref[:span, :] = score
        top_ref[...] = jnp.max(score.reshape(span // 8, 8, rows), axis=0)

    def fold_unit(unit, score_ref, top_ref, span):
        slot = unit % req_dev
        top = jnp.max(top_ref[...], axis=0, keepdims=True)
        expo = jnp.exp2((score_ref[:span, :] - top) * rate)
        total = jnp.sum(expo, axis=0, keepdims=True)
        added = jnp.dot(
            bands[req_dev + slot][:, :span],
            expo.astype(jnp.bfloat16),
            preferred_element_type=jnp.float32,
        )
        keep(unit, added, total)

    many = spread.shape[0] // tokens
    out_copies = []
    for at in range(0, heads, many):
        here = (slice(None), pl.ds(at, many), slice(None))
        out_copies.append(
            pltpu.make_async_copy(
                result_rows.at[here], out_hbm.at[here], sems.at[1 + len(out_copies)]
            )
        )

    def project(part):
        at = part * many
        for head in range(many):
            spread[pl.ds(head, tokens, stride=many), :] = jnp.dot(
                latent_out[at + head], value_up[at + head], preferred_element_type=jnp.float32
            )
        result_rows[:, at : at + many, :] = (
            spread[...].astype(jnp.bfloat16).reshape(tokens, many, result_rows.shape[2])
        )

    def run(span):
        def score_next(unit, score_ref, top_ref):
            if unit < req_dev:
                lay_band(unit, span)
            score_unit(unit, score_ref, top_ref, span)

        score_next(0, score_even, top_even)
        for unit in range(0, units - 2, 2):
            score_next(unit + 1, score_odd, top_odd)
            fold_unit(unit, score_even, top_even, span)
            score_next(unit + 2, score_even, top_even)
            fold_unit(unit + 1, score_odd, top_odd, span)
        score_unit(units - 1, score_odd, top_odd, span)
        fold_unit(units - 2, score_even, top_even, span)
        value_copy.wait()
        project(0)
        fold_unit(units - 1, score_odd, top_odd, span)
        out_copies[0].start()
        project(1)
        out_copies[1].start()

    def run_long(unit, carry):
        slot = lax.rem(unit, req_dev)

        def step(tile, state):
            top, total, added = state
            at = pl.ds(pl.multiple_of(tile * KEY_TILE, KEY_TILE), KEY_TILE)
            key_tile = keys_of(slot)[at, :]
            area = (KEY_TILE, LANES)
            bias_tile = seen(
                slot,
                lax.broadcasted_iota(jnp.int32, area, 0) + tile * KEY_TILE,
                jnp.bitwise_and(lax.broadcasted_iota(jnp.int32, area, 1), band - 1),
                starts,
                placed,
                owner,
                is_decode,
                tokens,
                band,
            )
            score = scored(unit, key_tile, bias_tile)
            now = jnp.maximum(top, jnp.max(score, axis=0, keepdims=True))
            shrink = jnp.exp2((top - now) * rate)
            expo = jnp.exp2((score - now) * rate)
            term = jnp.dot(
                key_tile[:, :rank].T, expo.astype(jnp.bfloat16), preferred_element_type=jnp.float32
            )
            total = total * shrink + jnp.sum(expo, axis=0, keepdims=True)
            return (now, total, added * shrink + term)

        state = (
            jnp.full((1, rows), masked_low, jnp.float32),
            jnp.zeros((1, rows), jnp.float32),
            jnp.zeros((rank, rows), jnp.float32),
        )
        top, total, added = lax.fori_loop(0, placed[slot * 5], step, state)
        keep(unit, added, total)
        return carry

    if compact:
        tiles = placed[0]
        for slot in range(1, req_dev):
            tiles = jnp.maximum(tiles, placed[slot * 5])
        for count in range(1, -(-most_keys // KEY_TILE) + 1):
            span = min(count * KEY_TILE, most_keys)
            pl.when(tiles == count)(functools.partial(run, span))
    else:
        lax.fori_loop(0, units, run_long, 0)
        value_copy.wait()
        for part, copy in enumerate(out_copies):
            project(part)
            copy.start()
    for copy in out_copies:
        copy.wait()


def key_room(tokens, tokens_all, band):
    longest = tokens_all // 2 + tokens
    most_keys = -(-(longest + ALIGN + band) // BLOCK) * BLOCK
    return most_keys, -(-most_keys // KEY_TILE) * KEY_TILE


def prepare_early(lengths, table, masks, pieces, tokens, tokens_all, width):
    req_dev = table.shape[0] // (tokens_all // tokens)
    groups = table.shape[0] // lengths.shape[0]
    room = key_room(tokens, tokens_all, tokens // req_dev)[1]
    small = pl.BlockSpec(memory_space=pltpu.SMEM)
    whole = pl.BlockSpec(memory_space=pltpu.VMEM)
    return pl.pallas_call(
        functools.partial(early_kernel, (masks, groups, req_dev, tokens, tokens_all)),
        in_specs=[small] * 2 + [whole] * len(pieces),
        out_specs=[whole, whole, small],
        out_shape=[
            jax.ShapeDtypeStruct((tokens_all + room, width), jnp.bfloat16),
            jax.ShapeDtypeStruct((req_dev, room, LANES), jnp.float32),
            jax.ShapeDtypeStruct((5 * req_dev,), jnp.int32),
        ],
        compiler_params=pltpu.CompilerParams(vmem_limit_bytes=12 << 20),
        name="early",
    )(lengths, table, *pieces)


def attend(
    lengths, table, queries, value_up, pieces, masks, own, other, tokens_all, nope_dim
):
    heads, tokens, width = queries.shape
    rank, v_dim = value_up.shape[1:]
    owners = tokens_all // tokens
    req_dev = table.shape[0] // owners
    groups = table.shape[0] // lengths.shape[0]
    band = tokens // req_dev
    longest = tokens_all // 2 + tokens
    most_keys, room = key_room(tokens, tokens_all, band)
    compact = most_keys <= 4 * KEY_TILE
    rate = math.log2(math.e) / math.sqrt(nope_dim + width - rank)
    group = 16
    many = heads // 2
    rows = group * band
    sizes = (masks, groups, req_dev, rank, rate, tokens_all, most_keys, group)
    small = pl.BlockSpec(memory_space=pltpu.SMEM)
    left = pl.BlockSpec(memory_space=pl.ANY)
    whole = pl.BlockSpec(memory_space=pltpu.VMEM)
    score = pltpu.VMEM((room if compact else KEY_TILE, rows), jnp.float32)
    top = pltpu.VMEM((8, rows), jnp.float32)
    if compact:
        bands = [pltpu.VMEM((room, width), jnp.bfloat16)] * req_dev
        bands += [pltpu.VMEM((rank, room), jnp.bfloat16)] * req_dev
    else:
        bands = [pltpu.VMEM((req_dev, room, width), jnp.bfloat16)]
        pieces = [*pieces, lengths, table]
    piece_specs = [whole] * (len(LATE) + 2) + [small] if compact else [left] * (len(pieces) - 2) + [small] * 2
    return pl.pallas_call(
        functools.partial(attend_kernel, sizes),
        in_specs=[whole, left] + piece_specs + [whole] * 2,
        out_specs=left,
        out_shape=jax.ShapeDtypeStruct((tokens, heads, v_dim), jnp.bfloat16),
        scratch_shapes=[
            pltpu.VMEM((tokens_all + (room if compact else 4 * KEY_TILE), width), jnp.bfloat16),
            pltpu.VMEM(value_up.shape, jnp.bfloat16),
            pltpu.VMEM((heads, tokens, rank), jnp.bfloat16),
            pltpu.VMEM((tokens * many, v_dim), jnp.float32),
            pltpu.VMEM((tokens, heads, v_dim), jnp.bfloat16),
            score,
            score,
            top,
            top,
            pltpu.SMEM((5 * req_dev,), jnp.int32),
            pltpu.SemaphoreType.DMA((1 + 2 * owners,)),
            *bands,
        ],
        compiler_params=pltpu.CompilerParams(vmem_limit_bytes=(36 if compact else 59) << 20),
        cost_estimate=pl.CostEstimate(
            flops=4 * heads * tokens * longest * width,
            bytes_accessed=2 * (value_up.size + heads * tokens * (width + v_dim)),
            transcendentals=heads * tokens * longest,
        ),
        name="attend",
    )(
        queries,
        pltpu.with_memory_space_constraint(value_up, pltpu.HBM),
        *pieces,
        own,
        other,
    )


def choose_kernel(own, handed, target):
    is_prefill = lax.axis_index("section") == 0
    rank = target.shape[1]

    def keep(source):
        if target.shape == source.shape:
            target[...] = source[...]
        else:
            target[:BLOCK, :] = source[:, :rank]
            target[BLOCK:, :] = packed_rope(source[:, rank:]).astype(jnp.bfloat16)

    pl.when(is_prefill)(functools.partial(keep, own))
    pl.when(jnp.logical_not(is_prefill))(functools.partial(keep, handed))


def join_kernel(first, second, target):
    if first.shape[0] % (BLOCK + 8):
        rows = first.shape[0]
        target[:rows, :] = first[...]
        target[rows:, :] = second[...]
    else:
        rows = first.shape[0] // (BLOCK + 8) * BLOCK
        target[:rows, :] = first[:rows, :]
        target[rows : 2 * rows, :] = second[:rows, :]
        ropes = [source[rows:, :].astype(jnp.float32) for source in (first, second)]
        target[2 * rows :, :] = jnp.concatenate(ropes, axis=0).astype(jnp.bfloat16)


def in_vmem(kernel, shape, *arrays):
    whole = pl.BlockSpec(memory_space=pltpu.VMEM)
    return pl.pallas_call(
        kernel,
        in_specs=[whole] * len(arrays),
        out_specs=whole,
        out_shape=jax.ShapeDtypeStruct(shape, arrays[0].dtype),
        compiler_params=pltpu.CompilerParams(vmem_limit_bytes=8 << 20),
        name="hold",
    )(*arrays)


def gathered(latent, absorb_part, early_part, rank):
    owners = lax.axis_size("seq")
    flip = lambda bit: [(owner, owner ^ bit) for owner in range(owners)]
    over = lambda chosen, bit: tuple(mask | bit for mask in chosen)
    swap = [(0, 1), (1, 0)]
    handed = lax.ppermute(
        latent, ("section", "seq"), [(owner, owners + (owner ^ 1)) for owner in range(owners)]
    )
    fresh = lax.ppermute(latent, "head", swap)
    block = latent.shape[0]
    queries, own = absorb_part(0, latent, None)
    handed, own, queries = lax.optimization_barrier((handed, own, queries))
    shape = latent.shape if early_part is None else (block + 8, rank)
    held = in_vmem(choose_kernel, shape, own, handed)
    masks = (0,)
    bit = owners // 2
    while bit > 2:
        received = lax.ppermute(held, "seq", flip(bit))
        if bit == owners // 2:
            queries = absorb_part(1, None, queries)[0]
            received, queries, fresh = lax.optimization_barrier((received, queries, fresh))
        held = in_vmem(join_kernel, (2 * held.shape[0], held.shape[1]), held, received)
        masks = masks + over(masks, bit)
        bit //= 2
    received = lax.ppermute(held, "seq", flip(2))
    swapped = lax.ppermute(held, "section", swap)
    held_other = lax.ppermute(held, "head", swap)
    crossed = lax.ppermute(received, "seq", flip(1))
    received_other = lax.ppermute(received, "head", swap)
    swapped_other = lax.ppermute(swapped, "head", swap)
    later = over(masks, 2)
    all_masks = (masks, later, over(masks, 1), over(later, 1))
    prepared = ()
    if early_part is not None:
        ready = [held, received, swapped, held_other]
        crossed, prepared = lax.optimization_barrier((crossed, early_part(all_masks, ready)))
    crossed_other = lax.ppermute(crossed, "head", swap)
    if early_part is not None:
        pieces = [received_other, swapped_other, crossed, crossed_other, *prepared]
    else:
        pieces = [held, received, swapped, crossed]
        pieces += [held_other, received_other, swapped_other, crossed_other]
    return pieces, all_masks, queries, fresh


def shards(query_nope, query_rope, latent, up_key, value_up_weight, lengths, owner_request_table):
    tokens_all = lax.axis_size("seq") * query_nope.shape[1]
    own = latent[0]
    share = query_nope.shape[2] // 2

    def absorb_part(part, carried, prior):
        first = part * share
        return absorb(query_nope[0], query_rope[0], up_key, 8, first, share, carried, prior)

    def early_part(masks, pieces):
        tokens, width = query_nope.shape[1], latent.shape[2]
        return prepare_early(
            lengths, owner_request_table, masks, pieces, tokens, tokens_all, width
        )

    compact = tokens_all <= 16 * BLOCK
    pieces, masks, queries, other = gathered(
        own, absorb_part, early_part if compact else None, up_key.shape[1]
    )
    attended = attend(
        lengths,
        owner_request_table,
        queries,
        value_up_weight,
        pieces,
        masks,
        own,
        other,
        tokens_all,
        query_nope.shape[3],
    )
    return attended[None]


def solution(mesh):
    in_specs = (
        P("section", "seq", "head", None),
        P("section", "seq", "head"),
        P("section", ("seq", "head"), None),
        P("head", None, None),
        P("head", None, None),
        P(),
        P(),
    )
    out_specs = P("section", "seq", "head", None)
    return jax.shard_map(shards, mesh=mesh, in_specs=in_specs, out_specs=out_specs, check_vma=False)
```
